128 devices in a mesh: stream: 32 (over y_hi, z, x), depth: 4 (over y_lo, core).
Axes of the slice: x: 4, y: 4 (y_hi: 2, y_lo: 2; y = y_hi * 2 + y_lo), z: 4, core: 2. Of those that a mesh axis runs over, the one named last changes fastest.
Arguments:
- populations: float32 [27, 128, 64, 128], P(None, 'stream', 'depth'), may hold values from 0 to 1, as said below
- moment_rates: float32 [27], replicated, may hold values from 0.6 to 1.9
- solid_bricks: int32 [32, 16, 32], P('stream', 'depth'), may hold values 0 or 1
- owners: int32 [16384, 1], P(('stream', 'depth')), may hold values from 0 to 127; in each aligned block of 128 rows (0 to 127, 128 to 255, ...) at most 2 rows name the same one
- bricks: int32 [16384], P(('stream', 'depth')), may hold values from 0 to 127
- levels: int32 [16384], P(('stream', 'depth')), may hold values from 1 to 2
Outputs:
- advanced: float32 [27, 128, 64, 128], P(None, 'stream', 'depth')
- ghosts: float32 [16384, 2, 1728], P(('stream', 'depth'))
The draws below stay inside these ranges and needn't reach their ends.
Inputs may be any that keep to these rules, and one draw needn't show every extreme that they name: `owners`: among the 128 entries of one device at most 2 name the same owner, and some device names some owner exactly 2 times. `populations`: populations are positive.
All inputs are finite; a program needn't handle non-finite values. No bound on the sum of `solid_bricks` on one device may be relied on, other than what follows from the above.
Results may differ from the reference program's by a relative error of at most 0.0001.
Values sent between devices are 32-bit elements; how exact they have to be, the bound alone decides.
A program may use at most 128 MiB of HBM per device.

```python
import math
import jax
import jax.numpy as jnp
import numpy as np
from jax import lax

BRICK = 4
CAP = 2
CX = 4
CY = 16
NZ = 128
NX = 128
NY = 64
BX = 32
BY = 16
BZ = 32
BDEV = 128
LIST = 128
N_STREAM = 32
N_DEPTH = 4


line_weights = np.array([1.0 / 6.0, 2.0 / 3.0, 1.0 / 6.0])


lattice_x = np.repeat(np.array([-1.0, 0.0, 1.0]), 9)


lattice_y = np.tile(np.repeat(np.array([-1.0, 0.0, 1.0]), 3), 3)


lattice_z = np.tile(np.array([-1.0, 0.0, 1.0]), 9)


lattice_weights = np.kron(np.kron(line_weights, line_weights), line_weights)


def draw_populations(key, part):
    keys = jax.random.split(jax.random.fold_in(key, 11), 4)
    density = jax.random.uniform(keys[0], (NX, NY, NZ), jnp.float32, 0.8, 1.2)
    velocity = jax.random.uniform(keys[1], (3, NX, NY, NZ), jnp.float32, -0.08, 0.08)
    noise = jax.random.uniform(keys[2], (27, NX, NY, NZ), jnp.float32, -0.15, 0.15)
    shape_col = (27, 1, 1, 1)
    along_x = jnp.asarray(lattice_x, jnp.float32).reshape(shape_col)
    along_y = jnp.asarray(lattice_y, jnp.float32).reshape(shape_col)
    along_z = jnp.asarray(lattice_z, jnp.float32).reshape(shape_col)
    weights = jnp.asarray(lattice_weights, jnp.float32).reshape(shape_col)
    projected = along_x * velocity[0] + along_y * velocity[1] + along_z * velocity[2]
    squared = jnp.sum(velocity * velocity, axis=0)
    balance = weights * density * (1.0 + 3.0 * projected + 4.5 * projected * projected - 1.5 * squared)
    return (balance * (1.0 + noise)).astype(jnp.float32)


def touch_ends(values, rng, least, high):
    spot = [jax.random.randint(jax.random.fold_in(rng, axis), (), 0, length) for axis, length in enumerate(values.shape)]
    widest = values.shape.index(max(values.shape))
    neighbour = spot[:widest] + [(spot[widest] + 1) % values.shape[widest]] + spot[widest + 1:]
    return values.at[tuple(spot)].set(least).at[tuple(neighbour)].set(high)


def deal_out(stream_key, own, number, rows, count, top, most, slope):
    order = jax.random.permutation(stream_key, count)
    heavy_load, usual = load_shares(count, rows * top, most, slope, True), load_shares(count, rows * top, most, slope, False)
    places = jnp.arange(count)

    def named(sizes, turn):
        used = int((sizes > 0).sum())
        fixed = max(1, used // 4)
        passed = fixed + (places - fixed + turn * (used - fixed)) % max(1, count - fixed)
        return jnp.zeros((count,), jnp.int32).at[order[jnp.where(places < fixed, places, passed)]].set(jnp.asarray(sizes, jnp.int32))

    sizes = jnp.where(number % 4 == 0, named(heavy_load, number // 4), named(usual, number - number // 4 - 1))
    mixed = jax.random.permutation(jax.random.fold_in(own, 3), count)
    source_of, sink = mixed[0:count // 2 * 2:2], mixed[1:count // 2 * 2:2]
    margin = jnp.minimum(sizes[source_of] - 1, most - sizes[sink]) // 2
    margin = jnp.where((source_of == order[0]) | (sink == order[0]) | (sizes[sink] == 0), 0, jnp.maximum(margin, 0))
    passed = jax.random.randint(jax.random.fold_in(own, 4), (count // 2,), 0, 1 << 20) % (margin + 1)
    sizes = sizes.at[source_of].add(-passed).at[sink].add(passed)
    items = jnp.searchsorted(jnp.cumsum(sizes), jnp.arange(rows * top), side="right").astype(jnp.int32)
    listing = items.reshape(top, rows).T
    listing = listing[jax.random.permutation(jax.random.fold_in(own, 1), rows)]
    turn = jax.random.randint(jax.random.fold_in(own, 2), (rows, 1), 0, top)
    return jnp.take_along_axis(listing, (jnp.arange(top)[None, :] + turn) % top, axis=1)


def load_shares(number_of, total, most, lean, full):
    portions = [(1 << 20) // math.isqrt(grade ** lean) + 1 for grade in range(1, number_of + 1)]
    largest = most if full else min(most, max(-(-total // number_of), total * portions[0] // sum(portions)))
    least = 1 if total - largest >= number_of - 1 else 0
    counts, surplus = [largest] + [least] * (number_of - 1), total - largest - least * (number_of - 1)
    while surplus > 0:
        candidates = [i for i in range(1, number_of) if counts[i] < largest] or [i for i in range(1, number_of) if counts[i] < most]
        whole, budget = sum([portions[i] for i in candidates]), surplus
        for i in candidates:
            more = min(most - counts[i], max(1, budget * portions[i] // whole), surplus)
            counts[i] = counts[i] + more
            surplus = surplus - more
    return np.array(counts)


def setup_inputs(seed: int = 0) -> dict:
    seeds = jax.random.split(jax.random.key(seed), 7)
    populations = draw_populations(jax.random.fold_in(seeds[6], 71), 0)
    moment_rates = jnp.clip(jax.random.uniform(seeds[1], (27,), jnp.float32, 0.6, 1.9), 0.6, 1.9)
    solid_bricks = touch_ends((jax.random.randint(seeds[2], (BX, BY, BZ), 0, 8) < 1).astype(jnp.int32), jax.random.fold_in(seeds[2], 1), 0, 1)
    owners_keys = jax.random.split(jax.random.fold_in(seeds[3], 1), (N_STREAM * N_DEPTH * LIST) // LIST)
    owners_turns = jax.random.permutation(jax.random.fold_in(seeds[3], 3), (N_STREAM * N_DEPTH * LIST) // LIST)
    owners = jax.vmap(lambda own, number: deal_out(jax.random.fold_in(seeds[3], 2), own, number, LIST, N_STREAM * N_DEPTH, 1, CAP, 2))(owners_keys, owners_turns).reshape((N_STREAM * N_DEPTH * LIST, 1))
    bricks = touch_ends(jax.random.randint(seeds[4], (N_STREAM * N_DEPTH * LIST,), 0, BDEV), jax.random.fold_in(seeds[4], 1), 0, BDEV - 1).astype(jnp.int32)
    levels = touch_ends(jax.random.randint(seeds[5], (N_STREAM * N_DEPTH * LIST,), 1, 3), jax.random.fold_in(seeds[5], 1), 1, 2).astype(jnp.int32)
    return {"populations": populations, "moment_rates": moment_rates, "solid_bricks": solid_bricks, "owners": owners, "bricks": bricks, "levels": levels}


power_table = np.array([[1.0, 1.0, 1.0], [-1.0, 0.0, 1.0], [1.0, 0.0, 1.0]])
inverse_table = np.array([[0.0, -0.5, 0.5], [1.0, 0.0, -1.0], [0.0, 0.5, 0.5]])
line_weights = np.array([1.0 / 6.0, 2.0 / 3.0, 1.0 / 6.0])
lattice_x = np.repeat(np.array([-1.0, 0.0, 1.0]), 9)
lattice_y = np.tile(np.repeat(np.array([-1.0, 0.0, 1.0]), 3), 3)
lattice_z = np.tile(np.array([-1.0, 0.0, 1.0]), 9)
lattice_weights = np.kron(np.kron(line_weights, line_weights), line_weights)


def equilibrium(popul):
    extra = popul.ndim - 1
    grouped = popul.reshape((3, 3, 3) + popul.shape[1:])
    density = jnp.sum(popul, axis=0)
    moment_x = jnp.sum(grouped[2], axis=(0, 1)) - jnp.sum(grouped[0], axis=(0, 1))
    moment_y = jnp.sum(grouped[:, 2], axis=(0, 1)) - jnp.sum(grouped[:, 0], axis=(0, 1))
    moment_z = jnp.sum(grouped[:, :, 2], axis=(0, 1)) - jnp.sum(grouped[:, :, 0], axis=(0, 1))
    speed_x = moment_x / density
    speed_y = moment_y / density
    speed_z = moment_z / density
    shape_col = (27,) + (1,) * extra
    along_x = jnp.asarray(lattice_x, jnp.float32).reshape(shape_col)
    along_y = jnp.asarray(lattice_y, jnp.float32).reshape(shape_col)
    along_z = jnp.asarray(lattice_z, jnp.float32).reshape(shape_col)
    weights = jnp.asarray(lattice_weights, jnp.float32).reshape(shape_col)
    projected = along_x * speed_x + along_y * speed_y + along_z * speed_z
    squared = speed_x * speed_x + speed_y * speed_y + speed_z * speed_z
    return weights * density * (1.0 + 3.0 * projected + 4.5 * projected * projected - 1.5 * squared)


def relax_matrix(moment_rates):
    moment = jnp.asarray(np.kron(np.kron(power_table, power_table), power_table), jnp.float32)
    inverse = jnp.asarray(np.kron(np.kron(inverse_table, inverse_table), inverse_table), jnp.float32)
    return jnp.dot(inverse * moment_rates[None, :], moment, precision=lax.Precision.HIGHEST)


def collide(flattened, solid_cells, relaxer):
    balance = equilibrium(flattened)
    relaxed = flattened - jnp.dot(relaxer, flattened - balance, precision=lax.Precision.HIGHEST)
    return jnp.where(solid_cells[None, :], flattened[::-1], relaxed)


def stream_global(collided):
    grouped = collided.reshape((3, 3, 3) + collided.shape[1:])
    pieces = []
    for along_x in range(3):
        for along_y in range(3):
            for along_z in range(3):
                pieces.append(jnp.roll(grouped[along_x, along_y, along_z], (along_x - 1, along_y - 1, along_z - 1), axis=(0, 1, 2)))
    return jnp.stack(pieces)


def rescale(chosen, levels, moment_rates):
    entries = chosen.shape[0]
    grouped = chosen.reshape(entries, 27, BRICK ** 3).transpose(1, 0, 2)
    balance = equilibrium(grouped)
    tau_coarse = 1.0 / moment_rates[12]
    spacing = jnp.where(levels == 2, 4.0, 2.0).astype(jnp.float32)
    tau_fine = 0.5 + spacing * (tau_coarse - 0.5)
    factor = (tau_fine / (spacing * tau_coarse))[None, :, None]
    fine_blocks = balance + factor * (grouped - balance)
    return fine_blocks.transpose(1, 0, 2).reshape(entries, 27 * BRICK ** 3)


def reference(populations, moment_rates, solid_bricks, owners, bricks, levels):
    relaxer = relax_matrix(moment_rates)
    cells_solid = jnp.repeat(jnp.repeat(jnp.repeat(solid_bricks, BRICK, 0), BRICK, 1), BRICK, 2) > 0
    current = populations

    def one_plane(pair):
        plane, mask_plane = pair
        flattened = plane.reshape(27, -1)
        return collide(flattened, mask_plane.reshape(-1), relaxer).reshape(plane.shape)

    for substep in range(2):
        planes = jnp.moveaxis(current, 1, 0)
        collided = jnp.moveaxis(lax.map(one_plane, (planes, cells_solid)), 0, 1)
        current = stream_global(collided)
    device_count = N_STREAM * N_DEPTH
    entries = device_count * LIST
    entry_index = jnp.arange(entries, dtype=jnp.int32)
    source = entry_index // LIST
    source_s = source // N_DEPTH
    source_p = source % N_DEPTH
    bricks_y = CY // BRICK
    local_x = bricks // (bricks_y * BZ)
    local_y = (bricks // BZ) % bricks_y
    local_z = bricks % BZ
    starts = jnp.stack([source_s * CX + local_x * BRICK, source_p * CY + local_y * BRICK, local_z * BRICK], axis=1).astype(jnp.int32)

    def take_block(start_row):
        zero_index = start_row[0] * 0
        return lax.dynamic_slice(current, (zero_index, start_row[0], start_row[1], start_row[2]), (27, BRICK, BRICK, BRICK)).reshape(-1)

    chosen = lax.map(take_block, starts)
    fine_blocks = rescale(chosen, levels, moment_rates)
    owner_rows = owners[:, 0].reshape(device_count, LIST)
    same_owner = owner_rows[:, :, None] == owner_rows[:, None, :]
    earlier = jnp.arange(LIST, dtype=jnp.int32)[None, :] < jnp.arange(LIST, dtype=jnp.int32)[:, None]
    slot_rank = jnp.sum((same_owner & earlier[None]).astype(jnp.int32), axis=2).reshape(entries)
    target = ((owners[:, 0] * device_count + source) * CAP + slot_rank).astype(jnp.int32)
    ghosts = jnp.zeros((device_count * device_count * CAP, 27 * BRICK ** 3), jnp.float32).at[target].set(fine_blocks)
    return current, ghosts.reshape(device_count * device_count, CAP, 27 * BRICK ** 3)
```

```python
import itertools
import random

import jax
import jax.numpy as jnp
import numpy as np
from jax import lax
from jax.experimental import pallas as pl
from jax.experimental.pallas import tpu as pltpu
from jax.sharding import PartitionSpec as P

MESH = pl.DeviceIdType.MESH
F32 = jnp.float32
BF16 = jnp.bfloat16

N_STREAM = 32
N_DEPTH = 4
N_DEV = N_STREAM * N_DEPTH
CX = 4
CY = 16
NZ = 128
TOP = 8
CHUNKS = 28

line = np.array([1.0 / 6.0, 2.0 / 3.0, 1.0 / 6.0])
power_table = np.array([[1.0, 1.0, 1.0], [-1.0, 0.0, 1.0], [1.0, 0.0, 1.0]])
VELOCITIES = list(itertools.product(range(3), repeat=3))


def equilibrium_terms():
    rows = []
    for a, b, c in VELOCITIES:
        w = line[a] * line[b] * line[c]
        x, y, z = a - 1.0, b - 1.0, c - 1.0
        square = [4.5 * x * x - 1.5, 4.5 * y * y - 1.5, 4.5 * z * z - 1.5]
        rows.append([w * t for t in [1.0, 3 * x, 3 * y, 3 * z] + square + [9 * x * y, 9 * x * z, 9 * y * z]])
    rows = np.array(rows)
    moments = np.kron(np.kron(power_table, power_table), power_table) @ rows
    return rows, np.where(np.abs(moments) < 1e-12, 0.0, moments)


GEQ_TERMS, MOMENT_TERMS = equilibrium_terms()


def combine(coefficients, basis):
    groups = {}
    for value, term in zip(coefficients, basis):
        if value != 0.0:
            groups.setdefault(round(float(value), 12), []).append(term)
    total = None
    for value, terms in groups.items():
        part = terms[0]
        for term in terms[1:]:
            part = part + term
        if value != 1.0:
            part = part * np.float32(value)
        total = part if total is None else total + part
    return total


def along(values, step):
    for axis in (2, 1, 0):
        out = {}
        for key in values:
            if key[axis] == 0:
                keys = [key[:axis] + (j,) + key[axis + 1:] for j in range(3)]
                for k, v in zip(keys, step(*[values[k] for k in keys])):
                    out[k] = v
        values = out
    return values


def to_moments(f0, f1, f2):
    ends = f0 + f2
    return ends + f1, f2 - f0, ends


def from_moments(m0, h1, h2):
    return h2 - h1, m0 - (h2 + h2), h2 + h1


def collide(f, solid, rate):
    moments = along(dict(zip(VELOCITIES, f)), to_moments)
    rho, jx, jy, jz = moments[0, 0, 0], moments[1, 0, 0], moments[0, 1, 0], moments[0, 0, 1]
    inverse = 1.0 / rho
    ux, uy, uz = jx * inverse, jy * inverse, jz * inverse
    basis = [rho, rho * ux, rho * uy, rho * uz, jx * ux, jy * uy, jz * uz, jx * uy, jx * uz, jy * uz]
    change = {}
    for k, key in enumerate(VELOCITIES):
        balance = combine(MOMENT_TERMS[k], basis)
        excess = moments[key] if balance is None else moments[key] - balance
        change[key] = excess * rate(k)
    change = along(change, from_moments)
    return [jnp.where(solid, f[26 - i], f[i] - change[key]) for i, key in enumerate(VELOCITIES)]


def rescaled(f, factors):
    rho = f[0]
    for value in f[1:]:
        rho = rho + value
    speeds = []
    for axis in range(3):
        up = [f[i] for i, v in enumerate(VELOCITIES) if v[axis] == 2]
        down = [f[i] for i, v in enumerate(VELOCITIES) if v[axis] == 0]
        total = up[0]
        for value in up[1:]:
            total = total + value
        for value in down:
            total = total - value
        speeds.append(total)
    inverse = 1.0 / rho
    jx, jy, jz = speeds
    ux, uy, uz = jx * inverse, jy * inverse, jz * inverse
    xx, yy, zz = jx * ux, jy * uy, jz * uz
    still = rho - 1.5 * (xx + yy + zz)
    out = [[None] * 27 for _ in factors]
    for i in range(14):
        a, b, c = (v - 1 for v in VELOCITIES[i])
        weight = np.float32(np.prod([line[v] for v in VELOCITIES[i]]))
        even, odd = still, None
        flow = None
        for sign, j, u in ((a, jx, ux), (b, jy, uy), (c, jz, uz)):
            if sign:
                flow = ((j, u) if sign > 0 else (-j, -u)) if flow is None else (
                    (flow[0] + j, flow[1] + u) if sign > 0 else (flow[0] - j, flow[1] - u))
        if flow is not None:
            even = still + 4.5 * (flow[0] * flow[1])
            odd = (3.0 * weight) * flow[0]
        even = even * weight
        for n, balance in ((i, even if odd is None else even + odd), (26 - i, even if odd is None else even - odd)):
            off = f[n] - balance
            for level, factor in enumerate(factors):
                out[level][n] = balance + factor * off
    return out


def offsets():
    every = [o for o in itertools.product(range(4), range(4), range(4), range(2)) if any(o)]
    random.Random(1).shuffle(every)
    return every


def advance(pop_ref, rates_ref, solid_ref, owners_ref, bricks_ref, levels_ref, adv_ref, got_ref,
            coll0, coll1, final, mask_ref, pick, fine, table_hi, table_lo, out_buf,
            halo_send, halo_recv, adv_sem, far_send, far_recv):
    s, p = lax.axis_index("stream"), lax.axis_index("depth")
    me = s * N_DEPTH + p
    x, y, z, core = s % 4, (s // 16) * 2 + p // 2, (s // 4) % 4, p % 2

    def place(offset):
        tx, ty, tz, tc = (x + offset[0]) % 4, (y + offset[1]) % 4, (z + offset[2]) % 4, (core + offset[3]) % 2
        return (ty // 2) * 16 + tz * 4 + tx, (ty % 2) * 2 + tc

    barrier = pltpu.get_barrier_semaphore()
    for offset in FAR:
        pl.semaphore_signal(barrier, inc=1, device_id=place(offset), device_id_type=MESH)

    spread = (lax.broadcasted_iota(jnp.int32, (32, NZ), 1) // 4 == lax.broadcasted_iota(jnp.int32, (32, NZ), 0)).astype(BF16)
    by_row = jnp.dot(solid_ref[...].astype(F32).astype(BF16), spread, preferred_element_type=F32)
    row = lax.broadcasted_iota(jnp.int32, (CY, NZ), 0) // 4
    mask = jnp.zeros((CY, NZ), F32)
    for b in range(CY // 4):
        mask = jnp.where(row == b, jnp.broadcast_to(by_row[b:b + 1, :], (CY, NZ)), mask)
    mask_ref[...] = mask

    def rate(k):
        halves = sum(1 for v in VELOCITIES[k] if v > 0)
        return rates_ref[k] * np.float32(0.5 ** halves)

    def moved(source, i, layer, half):
        a, b, c = VELOCITIES[i]
        value = source[a, b, c, layer + 2 - a, pl.ds(TOP + 8 * half + 1 - b, 8), :]
        return value if c == 1 else pltpu.roll(value, (c - 1) % NZ, 1)

    def collide_layer(layer, source, target):
        for half in range(2):
            rows = pl.ds(8 * half, 8)
            if source is None:
                f = [pop_ref[i, layer, rows, :] for i in range(27)]
            else:
                f = [moved(source, i, layer, half) for i in range(27)]
            for v, value in zip(VELOCITIES, collide(f, mask_ref[rows, :] > 0.5, rate)):
                target[v[0], v[1], v[2], layer + 1, pl.ds(TOP + 8 * half, 8), :] = value

    def halo(buf, step, n):
        dx, dy = HALO[n]
        first = {1: 2, -1: 0, 0: slice(None)}
        sx, lx = {1: (CX, 0), -1: (1, CX + 1), 0: (pl.ds(1, CX),) * 2}[dx]
        sy, ly = {1: (TOP + CY - 1, TOP - 1), -1: (TOP, TOP + CY), 0: (pl.ds(TOP, CY),) * 2}[dy]
        part = buf.at[first[dx], first[dy]] if dx and dy else (buf.at[first[dx]] if dx else buf.at[:, first[dy]])
        lead = (slice(None),) * (1 if dx and dy else 2)
        to = ((s + dx + N_STREAM) % N_STREAM, (p + dy + N_DEPTH) % N_DEPTH)
        return pltpu.make_async_remote_copy(
            part.at[lead + (sx, sy)], part.at[lead + (lx, ly)],
            halo_send.at[step, n], halo_recv.at[step, n], device_id=to, device_id_type=MESH)

    def sweep(layers, body):
        def once(t, _):
            body(layers(t))
            return 0
        lax.fori_loop(0, 2, once, 0)

    outer, inner = lambda t: 3 * t, lambda t: 1 + t

    sweep(outer, lambda layer: collide_layer(layer, None, coll0))
    pl.semaphore_wait(barrier, N_DEV - 1)
    for n in SIDE_X:
        halo(coll0, 0, n).start()
    sweep(inner, lambda layer: collide_layer(layer, None, coll0))
    for n in SIDE_Y:
        halo(coll0, 0, n).start()

    owner_row = jnp.broadcast_to(owners_ref[...], (N_DEV, N_DEV))
    owner_col = owner_row.T
    sub = lax.broadcasted_iota(jnp.int32, (N_DEV, N_DEV), 0)
    lane = lax.broadcasted_iota(jnp.int32, (N_DEV, N_DEV), 1)
    rank = jnp.sum(jnp.where((owner_row == owner_col) & (sub < lane), 1.0, 0.0), axis=0, keepdims=True)
    code = (bricks_ref[...] + 128 * levels_ref[...] - 127).astype(F32)
    for slot in range(2):
        named = jnp.where((owner_row == sub) & (rank == slot), jnp.broadcast_to(code, (N_DEV, N_DEV)), 0.0)
        taken = (4.0 * jnp.sum(named, axis=1, keepdims=True) - 4.0).astype(jnp.int32)
        for part in range(8):
            number = lane + 128 * part
            for zz in range(4):
                pick[pl.ds((zz * 2 + slot) * 128, 128), pl.ds(part * 128, 128)] = jnp.where(
                    number == taken + zz, 1.0, 0.0).astype(BF16)
    fine[:, :, pl.ds(432, 16), :] = jnp.zeros((2, 4, 16, NZ), F32)

    for n in SIDE_Y:
        halo(coll0, 0, n).wait_recv()
    sweep(inner, lambda layer: collide_layer(layer, coll0, coll1))
    for n in SIDE_X:
        halo(coll0, 0, n).wait_recv()
    sweep(outer, lambda layer: collide_layer(layer, coll0, coll1))
    for n in SIDE_X + SIDE_Y:
        halo(coll1, 1, n).start()

    tau = 1.0 / jnp.full((8, NZ), rates_ref[12], F32)
    factors = [(0.5 + h * (tau - 0.5)) / (h * tau) for h in (2.0, 4.0)]

    def finish(layer):
        for half in range(2):
            f = [moved(coll1, i, layer, half) for i in range(27)]
            for i in range(27):
                final[i, layer, pl.ds(8 * half, 8), :] = f[i]
            for level, values in enumerate(rescaled(f, factors)):
                for i in range(27):
                    for quarter in range(2):
                        fine[level, 2 * half + quarter, pl.ds(i * 16 + layer * 4, 4), :] = values[i][4 * quarter:4 * quarter + 4]

    for n in SIDE_Y:
        halo(coll1, 1, n).wait_recv()
    for layer in (1, 2):
        finish(layer)
    for n in SIDE_X:
        halo(coll1, 1, n).wait_recv()
    for layer in (0, 3):
        finish(layer)
    keep = pltpu.make_async_copy(final, adv_ref, adv_sem)
    keep.start()

    def far(part, offset):
        to = place(offset)
        return pltpu.make_async_remote_copy(
            out_buf.at[PARTS[part], to[0] * N_DEPTH + to[1]], got_ref.at[PARTS[part], me],
            far_send.at[part], far_recv.at[part], device_id=to, device_id_type=MESH)

    half_lane = lax.broadcasted_iota(jnp.int32, (N_DEV, 128), 1) < 64
    for part in range(4):
        if part < 3:
            rows = [pl.ds(part * 128, 128)]
        else:
            rows = [pl.ds(384, 64), pl.ds(384, 64)]
        highs, lows = [], []
        for piece in rows:
            high, low = [], []
            for level in range(2):
                for b in range(4):
                    value = fine[level, b, piece, :]
                    top = value.astype(BF16)
                    high.append(top)
                    low.append((value - top.astype(F32)).astype(BF16))
            highs.append(jnp.concatenate(high, axis=1))
            lows.append(jnp.concatenate(low, axis=1))
        table_hi[...] = jnp.concatenate(highs, axis=0)
        table_lo[...] = jnp.concatenate(lows, axis=0)
        dims = (((1,), (1,)), ((), ()))
        got = lax.dot_general(pick[...], table_hi[...], dims, preferred_element_type=F32)
        got = got + lax.dot_general(pick[...], table_lo[...], dims, preferred_element_type=F32)
        got = got.reshape(4, 2, N_DEV, 128)
        if part < 3:
            out_buf[pl.ds(part * 8, 8)] = got.reshape(8, N_DEV, 128)
        else:
            for zz in range(4):
                out_buf[24 + zz] = jnp.where(half_lane, got[zz, 0], got[zz, 1])
        for offset in FAR:
            far(part, offset).start()
        pltpu.make_async_copy(out_buf.at[PARTS[part], me], got_ref.at[PARTS[part], me], far_recv.at[part]).start()

    for step, buf in enumerate((coll0, coll1)):
        for n in SIDE_X + SIDE_Y:
            halo(buf, step, n).wait_send()
    keep.wait()
    for part in range(4):
        pltpu.make_async_copy(out_buf.at[PARTS[part]], got_ref.at[PARTS[part]], far_recv.at[part]).wait()
        rest = pl.ds(0, N_DEV - 1)
        pltpu.make_async_copy(out_buf.at[PARTS[part], rest], got_ref.at[PARTS[part], rest], far_send.at[part]).wait()


FAR = offsets()
HALO = [(1, 0), (-1, 0), (1, 1), (1, -1), (-1, 1), (-1, -1), (0, 1), (0, -1)]
SIDE_X = [0, 1, 2, 3, 4, 5]
SIDE_Y = [6, 7]
PARTS = [pl.ds(0, 8), pl.ds(8, 8), pl.ds(16, 8), pl.ds(24, 4)]


def arrange(adv_ref, got_ref, adv_out, ghosts_ref, sem):
    keep = pltpu.make_async_copy(adv_ref, adv_out, sem)
    keep.start()
    for part in range(4):
        for zz in range(4):
            for slot in range(2):
                base = slot * 1728 + part * 512 + zz
                if part < 3:
                    turned = got_ref[part * 8 + zz * 2 + slot].T
                    ghosts_ref[pl.ds(base, 128, stride=4), :] = turned
                elif slot == 0:
                    turned = got_ref[24 + zz].T
                    ghosts_ref[pl.ds(base, 48, stride=4), :] = turned[0:48]
                    ghosts_ref[pl.ds(base + 1728, 48, stride=4), :] = turned[64:112]
    keep.wait()


def per_device(populations, moment_rates, solid_bricks, owners, bricks, levels):
    vmem, hbm, smem = (pl.BlockSpec(memory_space=space) for space in (pltpu.VMEM, pl.ANY, pltpu.SMEM))
    padded = (3, 3, 3, CX + 2, CY + 16, NZ)
    adv, got = pl.pallas_call(
        advance,
        out_shape=(jax.ShapeDtypeStruct((27, CX, CY, NZ), F32), jax.ShapeDtypeStruct((CHUNKS, N_DEV, 128), F32)),
        in_specs=[vmem, smem, vmem, vmem, vmem, vmem],
        out_specs=(hbm, hbm),
        scratch_shapes=[
            pltpu.VMEM(padded, F32),
            pltpu.VMEM(padded, F32),
            pltpu.VMEM((27, CX, CY, NZ), F32),
            pltpu.VMEM((CY, NZ), F32),
            pltpu.VMEM((1024, 1024), BF16),
            pltpu.VMEM((2, 4, 448, NZ), F32),
            pltpu.VMEM((128, 1024), BF16),
            pltpu.VMEM((128, 1024), BF16),
            pltpu.VMEM((CHUNKS, N_DEV, 128), F32),
            pltpu.SemaphoreType.DMA((2, 8)),
            pltpu.SemaphoreType.DMA((2, 8)),
            pltpu.SemaphoreType.DMA,
            pltpu.SemaphoreType.DMA((4,)),
            pltpu.SemaphoreType.DMA((4,)),
        ],
        compiler_params=pltpu.CompilerParams(collective_id=0, has_side_effects=True, vmem_limit_bytes=40 << 20),
        name="advance",
    )(populations, moment_rates, solid_bricks.reshape(4, 32), owners.reshape(1, 128), bricks.reshape(1, 128), levels.reshape(1, 128))
    adv, ghosts = pl.pallas_call(
        arrange,
        out_shape=(jax.ShapeDtypeStruct((27, CX, CY, NZ), F32), jax.ShapeDtypeStruct((2 * 1728, N_DEV), F32)),
        in_specs=[hbm, vmem],
        out_specs=(hbm, vmem),
        scratch_shapes=[pltpu.SemaphoreType.DMA],
        compiler_params=pltpu.CompilerParams(vmem_limit_bytes=16 << 20),
        name="arrange",
    )(adv, got)
    return adv, ghosts.reshape(2, 1728, N_DEV).transpose(2, 0, 1)


def solution(mesh):
    return jax.shard_map(
        per_device,
        mesh=mesh,
        in_specs=(
            P(None, "stream", "depth", None),
            P(),
            P("stream", "depth", None),
            P(("stream", "depth"), None),
            P(("stream", "depth")),
            P(("stream", "depth")),
        ),
        out_specs=(P(None, "stream", "depth", None), P(("stream", "depth"), None, None)),
        check_vma=False,
    )
```

```python
import itertools
import random

import jax
import jax.numpy as jnp
import numpy as np
from jax import lax
from jax.experimental import pallas as pl
from jax.experimental.pallas import tpu as pltpu
from jax.sharding import PartitionSpec as P

LOGICAL = pl.DeviceIdType.LOGICAL
F32 = jnp.float32
BF16 = jnp.bfloat16

N_STREAM = 32
N_DEPTH = 4
N_DEV = N_STREAM * N_DEPTH
CX = 4
CY = 16
NZ = 128
TOP = 8
CHUNKS = 28

line = np.array([1.0 / 6.0, 2.0 / 3.0, 1.0 / 6.0])
power_table = np.array([[1.0, 1.0, 1.0], [-1.0, 0.0, 1.0], [1.0, 0.0, 1.0]])
VELOCITIES = list(itertools.product(range(3), repeat=3))


def equilibrium_terms():
    rows = []
    for a, b, c in VELOCITIES:
        w = line[a] * line[b] * line[c]
        x, y, z = a - 1.0, b - 1.0, c - 1.0
        square = [4.5 * x * x - 1.5, 4.5 * y * y - 1.5, 4.5 * z * z - 1.5]
        rows.append([w * t for t in [1.0, 3 * x, 3 * y, 3 * z] + square + [9 * x * y, 9 * x * z, 9 * y * z]])
    rows = np.array(rows)
    moments = np.kron(np.kron(power_table, power_table), power_table) @ rows
    return rows, np.where(np.abs(moments) < 1e-12, 0.0, moments)


GEQ_TERMS, MOMENT_TERMS = equilibrium_terms()


def combine(coefficients, basis):
    groups = {}
    for value, term in zip(coefficients, basis):
        if value != 0.0:
            groups.setdefault(round(float(value), 12), []).append(term)
    total = None
    for value, terms in groups.items():
        part = terms[0]
        for term in terms[1:]:
            part = part + term
        if value != 1.0:
            part = part * np.float32(value)
        total = part if total is None else total + part
    return total


def along(values, step):
    for axis in (2, 1, 0):
        out = {}
        for key in values:
            if key[axis] == 0:
                keys = [key[:axis] + (j,) + key[axis + 1:] for j in range(3)]
                for k, v in zip(keys, step(*[values[k] for k in keys])):
                    out[k] = v
        values = out
    return values


def to_moments(f0, f1, f2):
    ends = f0 + f2
    return ends + f1, f2 - f0, ends


def from_moments(m0, h1, h2):
    return h2 - h1, m0 - (h2 + h2), h2 + h1


def collide(f, solid, rate):
    moments = along(dict(zip(VELOCITIES, f)), to_moments)
    rho, jx, jy, jz = moments[0, 0, 0], moments[1, 0, 0], moments[0, 1, 0], moments[0, 0, 1]
    inverse = 1.0 / rho
    ux, uy, uz = jx * inverse, jy * inverse, jz * inverse
    basis = [rho, rho * ux, rho * uy, rho * uz, jx * ux, jy * uy, jz * uz, jx * uy, jx * uz, jy * uz]
    change = {}
    for k, key in enumerate(VELOCITIES):
        balance = combine(MOMENT_TERMS[k], basis)
        excess = moments[key] if balance is None else moments[key] - balance
        change[key] = excess * rate(k)
    change = along(change, from_moments)
    return [jnp.where(solid, f[26 - i], f[i] - change[key]) for i, key in enumerate(VELOCITIES)]


def rescaled(f, factors):
    rho = f[0]
    for value in f[1:]:
        rho = rho + value
    speeds = []
    for axis in range(3):
        up = [f[i] for i, v in enumerate(VELOCITIES) if v[axis] == 2]
        down = [f[i] for i, v in enumerate(VELOCITIES) if v[axis] == 0]
        total = up[0]
        for value in up[1:]:
            total = total + value
        for value in down:
            total = total - value
        speeds.append(total)
    inverse = 1.0 / rho
    jx, jy, jz = speeds
    ux, uy, uz = jx * inverse, jy * inverse, jz * inverse
    xx, yy, zz = jx * ux, jy * uy, jz * uz
    still = rho - 1.5 * (xx + yy + zz)
    out = [[None] * 27 for _ in factors]
    for i in range(14):
        a, b, c = (v - 1 for v in VELOCITIES[i])
        weight = np.float32(np.prod([line[v] for v in VELOCITIES[i]]))
        even, odd = still, None
        flow = None
        for sign, j, u in ((a, jx, ux), (b, jy, uy), (c, jz, uz)):
            if sign:
                flow = ((j, u) if sign > 0 else (-j, -u)) if flow is None else (
                    (flow[0] + j, flow[1] + u) if sign > 0 else (flow[0] - j, flow[1] - u))
        if flow is not None:
            even = still + 4.5 * (flow[0] * flow[1])
            odd = (3.0 * weight) * flow[0]
        even = even * weight
        for n, balance in ((i, even if odd is None else even + odd), (26 - i, even if odd is None else even - odd)):
            off = f[n] - balance
            for level, factor in enumerate(factors):
                out[level][n] = balance + factor * off
    return out


def hops(k):
    return sum((0, 1, 2, 1)[part] for part in ((k >> 2) & 3, (k >> 4) & 3, (k >> 1) & 1 | (k >> 5) & 2))


def others():
    every = list(range(1, N_DEV))
    random.Random(1).shuffle(every)
    return every


def advance(pop_hbm, rates_hbm, solid_hbm, owners_hbm, bricks_hbm, levels_hbm, adv_ref, got_ref,
            pop_ref, rates_ref, solid_ref, owners_ref, bricks_ref, levels_ref,
            coll0, coll1, final, mask_ref, pick, fine, table_hi, table_lo, out_buf,
            load_sem, halo_send, halo_recv, adv_sem, far_send, far_recv):
    loads = [pltpu.make_async_copy(pop_hbm.at[:, layer], pop_ref.at[:, layer], load_sem.at[layer]) for layer in range(CX)]
    small = [(rates_hbm, rates_ref), (solid_hbm, solid_ref), (owners_hbm, owners_ref), (bricks_hbm, bricks_ref), (levels_hbm, levels_ref)]
    loads += [pltpu.make_async_copy(a, b, load_sem.at[CX + i]) for i, (a, b) in enumerate(small)]
    for n in (4, 5, 0, 3, 1, 2, 6, 7, 8):
        loads[n].start()
    s, p = lax.axis_index("stream"), lax.axis_index("depth")
    me = s * N_DEPTH + p
    flips = [(1 << b) * (1 - 2 * ((me // (1 << b)) % 2)) for b in range(7)]
    low, high = [0], [me]
    for b in range(3):
        low = low + [t + flips[b] for t in low]
    for b in range(3, 7):
        high = high + [t + flips[b] for t in high]

    def place(k):
        return high[k >> 3] + low[k & 7]

    barrier = pltpu.get_barrier_semaphore()
    for k in sorted(FAR, key=lambda k: -hops(k)):
        pl.semaphore_signal(barrier, inc=1, device_id=place(k), device_id_type=LOGICAL)

    for n in (4, 5):
        loads[n].wait()
    spread = (lax.broadcasted_iota(jnp.int32, (32, NZ), 1) // 4 == lax.broadcasted_iota(jnp.int32, (32, NZ), 0)).astype(BF16)
    by_row = jnp.dot(solid_ref[...].astype(F32).astype(BF16), spread, preferred_element_type=F32)
    row = lax.broadcasted_iota(jnp.int32, (CY, NZ), 0) // 4
    mask = jnp.zeros((CY, NZ), F32)
    for b in range(CY // 4):
        mask = jnp.where(row == b, jnp.broadcast_to(by_row[b:b + 1, :], (CY, NZ)), mask)
    mask_ref[...] = mask

    def rate(k):
        halves = sum(1 for v in VELOCITIES[k] if v > 0)
        return rates_ref[k] * np.float32(0.5 ** halves)

    def moved(source, i, layer, half):
        a, b, c = VELOCITIES[i]
        value = source[a, b, c, layer + 2 - a, pl.ds(TOP + 8 * half + 1 - b, 8), :]
        return value if c == 1 else pltpu.roll(value, (c - 1) % NZ, 1)

    def collide_layer(layer, source, target):
        for half in range(2):
            rows = pl.ds(8 * half, 8)
            if source is None:
                f = [pop_ref[i, layer, rows, :] for i in range(27)]
            else:
                f = [moved(source, i, layer, half) for i in range(27)]
            for v, value in zip(VELOCITIES, collide(f, mask_ref[rows, :] > 0.5, rate)):
                target[v[0], v[1], v[2], layer + 1, pl.ds(TOP + 8 * half, 8), :] = value

    def halo(buf, step, n):
        dx, dy = HALO[n]
        first = {1: 2, -1: 0, 0: slice(None)}
        sx, lx = {1: (CX, 0), -1: (1, CX + 1), 0: (pl.ds(1, CX),) * 2}[dx]
        sy, ly = {1: (TOP + CY - 1, TOP - 1), -1: (TOP, TOP + CY), 0: (pl.ds(TOP, CY),) * 2}[dy]
        part = buf.at[first[dx], first[dy]] if dx and dy else (buf.at[first[dx]] if dx else buf.at[:, first[dy]])
        lead = (slice(None),) * (1 if dx and dy else 2)
        to = ((s + dx + N_STREAM) % N_STREAM) * N_DEPTH + (p + dy + N_DEPTH) % N_DEPTH
        return pltpu.make_async_remote_copy(
            part.at[lead + (sx, sy)], part.at[lead + (lx, ly)],
            halo_send.at[step, n], halo_recv.at[step, n], device_id=to, device_id_type=LOGICAL)

    def sweep(layers, body):
        def once(t, _):
            body(layers(t))
            return 0
        lax.fori_loop(0, 2, once, 0)

    outer, inner = lambda t: 3 * t, lambda t: 1 + t

    for n in (0, 3):
        loads[n].wait()
    sweep(outer, lambda layer: collide_layer(layer, None, coll0))
    pl.semaphore_wait(barrier, N_DEV - 1)
    for n in SIDE_X:
        halo(coll0, 0, n).start()
    for n in (1, 2):
        loads[n].wait()
    sweep(inner, lambda layer: collide_layer(layer, None, coll0))
    for n in SIDE_Y:
        halo(coll0, 0, n).start()

    for n in (6, 7, 8):
        loads[n].wait()
    owner_row = jnp.broadcast_to(owners_ref[...], (N_DEV, N_DEV))
    owner_col = owner_row.T
    sub = lax.broadcasted_iota(jnp.int32, (N_DEV, N_DEV), 0)
    lane = lax.broadcasted_iota(jnp.int32, (N_DEV, N_DEV), 1)
    rank = jnp.sum(jnp.where((owner_row == owner_col) & (sub < lane), 1.0, 0.0), axis=0, keepdims=True)
    code = (bricks_ref[...] + 128 * levels_ref[...] - 127).astype(F32)
    for slot in range(2):
        named = jnp.where((owner_row == sub) & (rank == slot), jnp.broadcast_to(code, (N_DEV, N_DEV)), 0.0)
        taken = (4.0 * jnp.sum(named, axis=1, keepdims=True) - 4.0).astype(jnp.int32)
        for part in range(8):
            number = lane + 128 * part
            for zz in range(4):
                pick[pl.ds((zz * 2 + slot) * 128, 128), pl.ds(part * 128, 128)] = jnp.where(
                    number == taken + zz, 1.0, 0.0).astype(BF16)
    fine[:, :, :, pl.ds(216, 40), :] = jnp.zeros((2, 2, 4, 40, NZ), F32)

    for n in SIDE_Y:
        halo(coll0, 0, n).wait_recv()
    sweep(inner, lambda layer: collide_layer(layer, coll0, coll1))
    for n in SIDE_X:
        halo(coll0, 0, n).wait_recv()
    sweep(outer, lambda layer: collide_layer(layer, coll0, coll1))
    for n in SIDE_X + SIDE_Y:
        halo(coll1, 1, n).start()

    tau = 1.0 / jnp.full((8, NZ), rates_ref[12], F32)
    factors = [(0.5 + h * (tau - 0.5)) / (h * tau) for h in (2.0, 4.0)]

    def finish(layer, side, which):
        for half in range(2):
            f = [moved(coll1, i, layer, half) for i in range(27)]
            for i in range(27):
                final[i, layer, pl.ds(8 * half, 8), :] = f[i]
            for level, values in enumerate(rescaled(f, factors)):
                for i in range(27):
                    for quarter in range(2):
                        fine[side, level, 2 * half + quarter, pl.ds(i * 8 + which * 4, 4), :] = values[i][4 * quarter:4 * quarter + 4]

    lanes = lax.broadcasted_iota(jnp.int32, (N_DEV, 128), 1)
    dims = (((1,), (1,)), ((), ()))

    def send(part):
        for k in FAR:
            to = place(k)
            pltpu.make_async_remote_copy(
                out_buf.at[PARTS[part], to], got_ref.at[PARTS[part], me],
                far_send.at[part], far_recv.at[part], device_id=to, device_id_type=LOGICAL).start()
        pltpu.make_async_copy(out_buf.at[PARTS[part], me], got_ref.at[PARTS[part], me], far_recv.at[part]).start()

    def hand_over(side):
        for level in range(2):
            for b in range(4):
                value = fine[side, level, b]
                top = value.astype(BF16)
                columns = pl.ds((level * 4 + b) * NZ, NZ)
                table_hi[:, columns] = top
                table_lo[:, columns] = (value - top.astype(F32)).astype(BF16)
        for pair in range(2):
            first = 14 * side + 6 * pair
            for zz in (2 * pair, 2 * pair + 1):
                chosen = pick[pl.ds(zz * 256, 256), :]
                got = lax.dot_general(chosen, table_hi[...], dims, preferred_element_type=F32)
                got = got + lax.dot_general(chosen, table_lo[...], dims, preferred_element_type=F32)
                slots = [got[0:128], got[128:256]]
                for slot in range(2):
                    out_buf[first + 2 * (zz % 2) + slot] = slots[slot][:, 0:128]
                rest = [value[:, 128:256] for value in slots]
                out_buf[first + 4 + zz % 2] = jnp.where(lanes < 64, rest[0], pltpu.roll(rest[1], 64, 1))
                for slot in range(2):
                    turned = pltpu.roll(rest[slot], (zz * 32 + 64) % 128, 1)
                    if zz:
                        turned = jnp.where(lanes // 32 == zz, turned, out_buf[14 * side + 12 + slot])
                    out_buf[14 * side + 12 + slot] = turned
            send(2 * side + pair)

    for n in SIDE_Y:
        halo(coll1, 1, n).wait_recv()
    finish(1, 0, 0)
    finish(2, 0, 1)
    hand_over(0)
    for n in SIDE_X:
        halo(coll1, 1, n).wait_recv()
    finish(0, 1, 0)
    finish(3, 1, 1)
    keep = pltpu.make_async_copy(final, adv_ref, adv_sem)
    keep.start()
    hand_over(1)

    for step, buf in enumerate((coll0, coll1)):
        for n in SIDE_X + SIDE_Y:
            halo(buf, step, n).wait_send()
    keep.wait()
    for part in range(4):
        pltpu.make_async_copy(out_buf.at[PARTS[part]], got_ref.at[PARTS[part]], far_recv.at[part]).wait()
        rest = pl.ds(0, N_DEV - 1)
        pltpu.make_async_copy(out_buf.at[PARTS[part], rest], got_ref.at[PARTS[part], rest], far_send.at[part]).wait()


FAR = others()
HALO = [(1, 0), (-1, 0), (1, 1), (1, -1), (-1, 1), (-1, -1), (0, 1), (0, -1)]
SIDE_X = [0, 1, 2, 3, 4, 5]
SIDE_Y = [6, 7]
PARTS = [pl.ds(0, 6), pl.ds(6, 8), pl.ds(14, 6), pl.ds(20, 8)]


def arrange(adv_ref, got_hbm, adv_out, ghosts_hbm, got_ref, ghosts_ref, kept_ref, keep_sem, load_sem, store_sem):
    loads = [pltpu.make_async_copy(got_hbm.at[rows], got_ref.at[rows], load_sem.at[part]) for part, rows in enumerate(PARTS)]
    for load in loads:
        load.start()
    fetch = pltpu.make_async_copy(adv_ref, kept_ref, keep_sem.at[0])
    fetch.start()

    def put(turned, first, slot, velocities, side, zz):
        for n, i in enumerate(velocities):
            start, base = first + n * 8, slot * 1728 + i * 64 + zz
            if side == 0:
                ghosts_ref[pl.ds(base + 16, 8, stride=4), :] = turned[start:start + 8]
            else:
                ghosts_ref[pl.ds(base, 4, stride=4), :] = turned[start:start + 4]
                ghosts_ref[pl.ds(base + 48, 4, stride=4), :] = turned[start + 4:start + 8]

    for part in range(4):
        loads[part].wait()
        side, pair = part // 2, part % 2
        first = 14 * side + 6 * pair
        for zz in (2 * pair, 2 * pair + 1):
            for slot in range(2):
                put(got_ref[first + 2 * (zz % 2) + slot].T, 0, slot, range(16), side, zz)
            turned = got_ref[first + 4 + zz % 2].T
            for slot in range(2):
                put(turned, 64 * slot, slot, range(16, 24), side, zz)
        if pair == 1:
            for slot in range(2):
                turned = got_ref[14 * side + 12 + slot].T
                for zz in range(4):
                    put(turned, 32 * zz, slot, range(24, 27), side, zz)
    fetch.wait()
    stores = [pltpu.make_async_copy(kept_ref, adv_out, keep_sem.at[1]), pltpu.make_async_copy(ghosts_ref, ghosts_hbm, store_sem)]
    for store in stores:
        store.start()
    for store in stores:
        store.wait()


def per_device(populations, moment_rates, solid_bricks, owners, bricks, levels):
    hbm = pl.BlockSpec(memory_space=pl.ANY)
    padded = (3, 3, 3, CX + 2, CY + 16, NZ)
    adv, got = pl.pallas_call(
        advance,
        out_shape=(jax.ShapeDtypeStruct((27, CX, CY, NZ), F32), jax.ShapeDtypeStruct((CHUNKS, N_DEV, 128), F32)),
        in_specs=[hbm] * 6,
        out_specs=(hbm, hbm),
        scratch_shapes=[
            pltpu.VMEM((27, CX, CY, NZ), F32),
            pltpu.SMEM((27,), F32),
            pltpu.VMEM((4, 32), jnp.int32),
            pltpu.VMEM((1, 128), jnp.int32),
            pltpu.VMEM((1, 128), jnp.int32),
            pltpu.VMEM((1, 128), jnp.int32),
            pltpu.VMEM(padded, F32),
            pltpu.VMEM(padded, F32),
            pltpu.VMEM((27, CX, CY, NZ), F32),
            pltpu.VMEM((CY, NZ), F32),
            pltpu.VMEM((1024, 1024), BF16),
            pltpu.VMEM((2, 2, 4, 256, NZ), F32),
            pltpu.VMEM((256, 1024), BF16),
            pltpu.VMEM((256, 1024), BF16),
            pltpu.VMEM((CHUNKS, N_DEV, 128), F32),
            pltpu.SemaphoreType.DMA((CX + 5,)),
            pltpu.SemaphoreType.DMA((2, 8)),
            pltpu.SemaphoreType.DMA((2, 8)),
            pltpu.SemaphoreType.DMA,
            pltpu.SemaphoreType.DMA((4,)),
            pltpu.SemaphoreType.DMA((4,)),
        ],
        compiler_params=pltpu.CompilerParams(collective_id=0, has_side_effects=True, vmem_limit_bytes=60 << 20),
        name="advance",
    )(populations, moment_rates, solid_bricks.reshape(4, 32), owners.reshape(1, 128), bricks.reshape(1, 128), levels.reshape(1, 128))
    adv, ghosts = pl.pallas_call(
        arrange,
        out_shape=(jax.ShapeDtypeStruct((27, CX, CY, NZ), F32), jax.ShapeDtypeStruct((2 * 1728, N_DEV), F32)),
        in_specs=[hbm, hbm],
        out_specs=(hbm, hbm),
        scratch_shapes=[
            pltpu.VMEM((CHUNKS, N_DEV, 128), F32),
            pltpu.VMEM((2 * 1728, N_DEV), F32),
            pltpu.VMEM((27, CX, CY, NZ), F32),
            pltpu.SemaphoreType.DMA((2,)),
            pltpu.SemaphoreType.DMA((4,)),
            pltpu.SemaphoreType.DMA,
        ],
        compiler_params=pltpu.CompilerParams(vmem_limit_bytes=60 << 20),
        name="arrange",
    )(adv, got)
    return adv, ghosts.reshape(2, 1728, N_DEV).transpose(2, 0, 1)


def solution(mesh):
    return jax.shard_map(
        per_device,
        mesh=mesh,
        in_specs=(
            P(None, "stream", "depth", None),
            P(),
            P("stream", "depth", None),
            P(("stream", "depth"), None),
            P(("stream", "depth")),
            P(("stream", "depth")),
        ),
        out_specs=(P(None, "stream", "depth", None), P(("stream", "depth"), None, None)),
        check_vma=False,
    )
```

```python
import itertools
import random

import jax
import jax.numpy as jnp
import numpy as np
from jax import lax
from jax.experimental import pallas as pl
from jax.experimental.pallas import tpu as pltpu
from jax.sharding import PartitionSpec as P

LOGICAL = pl.DeviceIdType.LOGICAL
F32 = jnp.float32
BF16 = jnp.bfloat16

N_STREAM = 32
N_DEPTH = 4
N_DEV = N_STREAM * N_DEPTH
CX = 4
CY = 16
NZ = 128
TOP = 8
CHUNKS = 27

line = np.array([1.0 / 6.0, 2.0 / 3.0, 1.0 / 6.0])
power_table = np.array([[1.0, 1.0, 1.0], [-1.0, 0.0, 1.0], [1.0, 0.0, 1.0]])
VELOCITIES = list(itertools.product(range(3), repeat=3))


def equilibrium_terms():
    rows = []
    for a, b, c in VELOCITIES:
        w = line[a] * line[b] * line[c]
        x, y, z = a - 1.0, b - 1.0, c - 1.0
        square = [4.5 * x * x - 1.5, 4.5 * y * y - 1.5, 4.5 * z * z - 1.5]
        rows.append([w * t for t in [1.0, 3 * x, 3 * y, 3 * z] + square + [9 * x * y, 9 * x * z, 9 * y * z]])
    rows = np.array(rows)
    moments = np.kron(np.kron(power_table, power_table), power_table) @ rows
    return rows, np.where(np.abs(moments) < 1e-12, 0.0, moments)


GEQ_TERMS, MOMENT_TERMS = equilibrium_terms()


def combine(coefficients, basis):
    groups = {}
    for value, term in zip(coefficients, basis):
        if value != 0.0:
            groups.setdefault(round(float(value), 12), []).append(term)
    total = None
    for value, terms in groups.items():
        part = terms[0]
        for term in terms[1:]:
            part = part + term
        if value != 1.0:
            part = part * np.float32(value)
        total = part if total is None else total + part
    return total


def along(values, step):
    for axis in (2, 1, 0):
        out = {}
        for key in values:
            if key[axis] == 0:
                keys = [key[:axis] + (j,) + key[axis + 1:] for j in range(3)]
                for k, v in zip(keys, step(*[values[k] for k in keys])):
                    out[k] = v
        values = out
    return values


def to_moments(f0, f1, f2):
    ends = f0 + f2
    return ends + f1, f2 - f0, ends


def from_moments(m0, h1, h2):
    return h2 - h1, m0 - (h2 + h2), h2 + h1


def collide(f, solid, rate):
    moments = along(dict(zip(VELOCITIES, f)), to_moments)
    rho, jx, jy, jz = moments[0, 0, 0], moments[1, 0, 0], moments[0, 1, 0], moments[0, 0, 1]
    inverse = 1.0 / rho
    ux, uy, uz = jx * inverse, jy * inverse, jz * inverse
    basis = [rho, rho * ux, rho * uy, rho * uz, jx * ux, jy * uy, jz * uz, jx * uy, jx * uz, jy * uz]
    change = {}
    for k, key in enumerate(VELOCITIES):
        balance = combine(MOMENT_TERMS[k], basis)
        excess = moments[key] if balance is None else moments[key] - balance
        change[key] = excess * rate(k)
    change = along(change, from_moments)
    return [jnp.where(solid, f[26 - i], f[i] - change[key]) for i, key in enumerate(VELOCITIES)]


def rescaled(f, factors):
    rho = f[0]
    for value in f[1:]:
        rho = rho + value
    speeds = []
    for axis in range(3):
        up = [f[i] for i, v in enumerate(VELOCITIES) if v[axis] == 2]
        down = [f[i] for i, v in enumerate(VELOCITIES) if v[axis] == 0]
        total = up[0]
        for value in up[1:]:
            total = total + value
        for value in down:
            total = total - value
        speeds.append(total)
    inverse = 1.0 / rho
    jx, jy, jz = speeds
    ux, uy, uz = jx * inverse, jy * inverse, jz * inverse
    xx, yy, zz = jx * ux, jy * uy, jz * uz
    still = rho - 1.5 * (xx + yy + zz)
    out = [[None] * 27 for _ in factors]
    for i in range(14):
        a, b, c = (v - 1 for v in VELOCITIES[i])
        weight = np.float32(np.prod([line[v] for v in VELOCITIES[i]]))
        even, odd = still, None
        flow = None
        for sign, j, u in ((a, jx, ux), (b, jy, uy), (c, jz, uz)):
            if sign:
                flow = ((j, u) if sign > 0 else (-j, -u)) if flow is None else (
                    (flow[0] + j, flow[1] + u) if sign > 0 else (flow[0] - j, flow[1] - u))
        if flow is not None:
            even = still + 4.5 * (flow[0] * flow[1])
            odd = (3.0 * weight) * flow[0]
        even = even * weight
        for n, balance in ((i, even if odd is None else even + odd), (26 - i, even if odd is None else even - odd)):
            off = f[n] - balance
            for level, factor in enumerate(factors):
                out[level][n] = balance + factor * off
    return out


def hops(k):
    return sum((0, 1, 2, 1)[part] for part in ((k >> 2) & 3, (k >> 4) & 3, (k >> 1) & 1 | (k >> 5) & 2))


def others():
    every = list(range(1, N_DEV))
    random.Random(1).shuffle(every)
    return every


def advance(pop_hbm, rates_hbm, solid_hbm, owners_hbm, bricks_hbm, levels_hbm, adv_ref, got_ref,
            pop_ref, rates_ref, solid_ref, owners_ref, bricks_ref, levels_ref,
            coll0, coll1, final, mask_ref, pick, fine, table_hi, table_lo, out_buf,
            load_sem, halo_send, halo_recv, adv_sem, far_send, far_recv):
    loads = [pltpu.make_async_copy(pop_hbm.at[:, layer], pop_ref.at[:, layer], load_sem.at[layer]) for layer in range(CX)]
    small = [(rates_hbm, rates_ref), (solid_hbm, solid_ref), (owners_hbm, owners_ref), (bricks_hbm, bricks_ref), (levels_hbm, levels_ref)]
    loads += [pltpu.make_async_copy(a, b, load_sem.at[CX + i]) for i, (a, b) in enumerate(small)]
    for n in (4, 5, 0, 3, 1, 2, 6, 7, 8):
        loads[n].start()
    s, p = lax.axis_index("stream"), lax.axis_index("depth")
    me = s * N_DEPTH + p
    flips = [(1 << b) * (1 - 2 * ((me // (1 << b)) % 2)) for b in range(7)]
    low, high = [0], [me]
    for b in range(3):
        low = low + [t + flips[b] for t in low]
    for b in range(3, 7):
        high = high + [t + flips[b] for t in high]

    def place(k):
        return high[k >> 3] + low[k & 7]

    barrier = pltpu.get_barrier_semaphore()
    for k in sorted(FAR, key=lambda k: -hops(k)):
        pl.semaphore_signal(barrier, inc=1, device_id=place(k), device_id_type=LOGICAL)

    for n in (4, 5):
        loads[n].wait()
    spread = (lax.broadcasted_iota(jnp.int32, (32, NZ), 1) // 4 == lax.broadcasted_iota(jnp.int32, (32, NZ), 0)).astype(BF16)
    by_row = jnp.dot(solid_ref[...].astype(F32).astype(BF16), spread, preferred_element_type=F32)
    row = lax.broadcasted_iota(jnp.int32, (CY, NZ), 0) // 4
    mask = jnp.zeros((CY, NZ), F32)
    for b in range(CY // 4):
        mask = jnp.where(row == b, jnp.broadcast_to(by_row[b:b + 1, :], (CY, NZ)), mask)
    mask_ref[pl.ds(0, CY), :] = mask

    def rate(k):
        halves = sum(1 for v in VELOCITIES[k] if v > 0)
        return rates_ref[k] * np.float32(0.5 ** halves)

    def moved(source, i, layer, half):
        a, b, c = VELOCITIES[i]
        value = source[a, b, c, layer + 2 - a, pl.ds(TOP + 8 * half + 1 - b, 8), :]
        return value if c == 1 else pltpu.roll(value, (c - 1) % NZ, 1)

    def collide_layer(layer, source, target):
        for half in range(2):
            rows = pl.ds(8 * half, 8)
            if source is None:
                f = [pop_ref[i, layer, rows, :] for i in range(27)]
            else:
                f = [moved(source, i, layer, half) for i in range(27)]
            for v, value in zip(VELOCITIES, collide(f, mask_ref[rows, :] > 0.5, rate)):
                target[v[0], v[1], v[2], layer + 1, pl.ds(TOP + 8 * half, 8), :] = value

    def halo(step, n):
        dx, dy = HALO[n]
        buf, deep = (coll0, 2) if step == 0 else (coll1, 1)
        sx, lx = {1: (CX, 0), -1: (1, CX + 1), 0: (pl.ds(1, CX),) * 2}[dx]
        sy, ly = {1: (TOP + CY - deep, TOP - deep), -1: (TOP, TOP + CY), 0: (TOP,) * 2}[dy]
        rows = CY if dy == 0 else deep
        a = {1: pl.ds(2, 1), -1: pl.ds(0, 1), 0: slice(None)}[dx]
        b = {1: pl.ds(3 - deep, deep), -1: pl.ds(0, deep), 0: slice(None)}[dy]
        to = ((s + dx + N_STREAM) % N_STREAM) * N_DEPTH + (p + dy + N_DEPTH) % N_DEPTH
        return pltpu.make_async_remote_copy(
            buf.at[a, b, :, sx, pl.ds(sy, rows)], buf.at[a, b, :, lx, pl.ds(ly, rows)],
            halo_send.at[step, n], halo_recv.at[step, n], device_id=to, device_id_type=LOGICAL)

    def mask_row(n):
        dy = HALO[n][1]
        to = s * N_DEPTH + (p + dy + N_DEPTH) % N_DEPTH
        return pltpu.make_async_remote_copy(
            mask_ref.at[pl.ds(CY - 1 if dy > 0 else 0, 1)], mask_ref.at[pl.ds(CY if dy > 0 else CY + 1, 1)],
            halo_send.at[1, n], halo_recv.at[1, n], device_id=to, device_id_type=LOGICAL)

    def collide_edges():
        f = []
        for a, b, c in VELOCITIES:
            value = jnp.concatenate(
                [coll0[a, b, c, layer + 2 - a, pl.ds(TOP - b, 2, stride=CY + 1), :] for layer in range(CX)], axis=0)
            f.append(value if c == 1 else pltpu.roll(value, (c - 1) % NZ, 1))
        solid = jnp.concatenate([mask_ref[pl.ds(CY, 2), :]] * CX, axis=0)
        for (a, b, c), value in zip(VELOCITIES, collide(f, solid > 0.5, rate)):
            if b != 1:
                side = 0 if b == 2 else 1
                for layer in range(CX):
                    row = 2 * layer + side
                    coll1[a, b, c, layer + 1, pl.ds(TOP + CY if side else TOP - 1, 1), :] = value[row:row + 1]

    def sweep(layers, body):
        def once(t, _):
            body(layers(t))
            return 0
        lax.fori_loop(0, 2, once, 0)

    outer, inner = lambda t: 3 * t, lambda t: 1 + t

    for n in (0, 3):
        loads[n].wait()
    sweep(outer, lambda layer: collide_layer(layer, None, coll0))
    pl.semaphore_wait(barrier, N_DEV - 1)
    for n in SIDE_X:
        halo(0, n).start()
    for n in (1, 2):
        loads[n].wait()
    sweep(inner, lambda layer: collide_layer(layer, None, coll0))
    for n in SIDE_Y:
        mask_row(n).start()
        halo(0, n).start()

    for n in (6, 7, 8):
        loads[n].wait()
    owner_row = jnp.broadcast_to(owners_ref[...], (N_DEV, N_DEV))
    owner_col = owner_row.T
    sub = lax.broadcasted_iota(jnp.int32, (N_DEV, N_DEV), 0)
    lane = lax.broadcasted_iota(jnp.int32, (N_DEV, N_DEV), 1)
    rank = jnp.sum(jnp.where((owner_row == owner_col) & (sub < lane), 1.0, 0.0), axis=0, keepdims=True)
    code = (bricks_ref[...] + 128 * levels_ref[...] - 127).astype(F32)
    for slot in range(2):
        named = jnp.where((owner_row == sub) & (rank == slot), jnp.broadcast_to(code, (N_DEV, N_DEV)), 0.0)
        taken = (4.0 * jnp.sum(named, axis=1, keepdims=True) - 4.0).astype(jnp.int32)
        for part in range(8):
            number = lane + 128 * part
            for zz in range(4):
                pick[pl.ds((zz * 2 + slot) * 128, 128), pl.ds(part * 128, 128)] = jnp.where(
                    number == taken + zz, 1.0, 0.0).astype(BF16)
    fine[:, :, :, pl.ds(216, 40), :] = jnp.zeros((2, 2, 4, 40, NZ), F32)

    for n in SIDE_Y:
        mask_row(n).wait_recv()
        halo(0, n).wait_recv()
    sweep(inner, lambda layer: collide_layer(layer, coll0, coll1))
    for n in SIDE_X:
        halo(0, n).wait_recv()
    sweep(outer, lambda layer: collide_layer(layer, coll0, coll1))
    for n in SIDE_X:
        halo(1, n).start()
    collide_edges()

    tau = 1.0 / jnp.full((8, NZ), rates_ref[12], F32)
    factors = [(0.5 + h * (tau - 0.5)) / (h * tau) for h in (2.0, 4.0)]

    def finish(layer, side, which):
        for half in range(2):
            f = [moved(coll1, i, layer, half) for i in range(27)]
            for i in range(27):
                final[i, layer, pl.ds(8 * half, 8), :] = f[i]
            for level, values in enumerate(rescaled(f, factors)):
                for i in range(27):
                    for quarter in range(2):
                        fine[side, level, 2 * half + quarter, pl.ds(i * 8 + which * 4, 4), :] = values[i][4 * quarter:4 * quarter + 4]

    lanes = lax.broadcasted_iota(jnp.int32, (N_DEV, 128), 1)
    dims = (((1,), (1,)), ((), ()))

    def send(part):
        for k in FAR:
            to = place(k)
            pltpu.make_async_remote_copy(
                out_buf.at[PARTS[part], to], got_ref.at[PARTS[part], me],
                far_send.at[part], far_recv.at[part], device_id=to, device_id_type=LOGICAL).start()
        pltpu.make_async_copy(out_buf.at[PARTS[part], me], got_ref.at[PARTS[part], me], far_recv.at[part]).start()

    def hand_over(side):
        for level in range(2):
            for b in range(4):
                value = fine[side, level, b]
                top = value.astype(BF16)
                columns = pl.ds((level * 4 + b) * NZ, NZ)
                table_hi[:, columns] = top
                table_lo[:, columns] = (value - top.astype(F32)).astype(BF16)
        for pair in range(2):
            part = 2 * side + pair
            for zz in (2 * pair, 2 * pair + 1):
                chosen = pick[pl.ds(zz * 256, 256), :]
                got = lax.dot_general(chosen, table_hi[...], dims, preferred_element_type=F32)
                got = got + lax.dot_general(chosen, table_lo[...], dims, preferred_element_type=F32)
                for slot in range(2):
                    value = got[128 * slot:128 * slot + 128]
                    out_buf[whole(side, zz, slot)] = value[:, 0:128]
                    place_at = 88 * (side * 8 + zz * 2 + slot)
                    chunk, start = place_at // 128, place_at % 128
                    turned = value[:, 128:256]
                    if start:
                        turned = pltpu.roll(turned, start, 1)
                        out_buf[mixed(chunk)] = jnp.where(lanes < start, out_buf[mixed(chunk)], turned)
                    else:
                        out_buf[mixed(chunk)] = turned
                    if start + 88 > 128:
                        out_buf[mixed(chunk + 1)] = turned
            send(part)

    finish(1, 0, 0)
    finish(2, 0, 1)
    hand_over(0)
    for n in SIDE_X:
        halo(1, n).wait_recv()
    finish(0, 1, 0)
    finish(3, 1, 1)
    keep = pltpu.make_async_copy(final, adv_ref, adv_sem)
    keep.start()
    hand_over(1)

    for n in SIDE_X:
        halo(0, n).wait_send()
        halo(1, n).wait_send()
    for n in SIDE_Y:
        halo(0, n).wait_send()
        mask_row(n).wait_send()
    keep.wait()
    for part in range(4):
        pltpu.make_async_copy(out_buf.at[PARTS[part]], got_ref.at[PARTS[part]], far_recv.at[part]).wait()
        rest = pl.ds(0, N_DEV - 1)
        pltpu.make_async_copy(out_buf.at[PARTS[part], rest], got_ref.at[PARTS[part], rest], far_send.at[part]).wait()


FAR = others()
HALO = [(1, 0), (-1, 0), (1, 1), (1, -1), (-1, 1), (-1, -1), (0, 1), (0, -1)]
SIDE_X = [0, 1, 2, 3, 4, 5]
SIDE_Y = [6, 7]
FIRST = [0, 6, 13, 20, CHUNKS]
PARTS = [pl.ds(a, b - a) for a, b in zip(FIRST, FIRST[1:])]


def whole(side, zz, slot):
    return FIRST[2 * side + zz // 2] + zz % 2 * 2 + slot


def mixed(n):
    return ([4, 5] + [10, 11, 12] + [17, 18, 19] + [24, 25, 26])[n]


def arrange(adv_ref, got_hbm, adv_out, ghosts_hbm, got_ref, ghosts_ref, kept_ref, keep_sem, load_sem, store_sem):
    loads = [pltpu.make_async_copy(got_hbm.at[rows], got_ref.at[rows], load_sem.at[part]) for part, rows in enumerate(PARTS)]
    for load in loads:
        load.start()
    fetch = pltpu.make_async_copy(adv_ref, kept_ref, keep_sem.at[0])
    fetch.start()

    def put(eight, i, side, zz, slot):
        base = slot * 1728 + i * 64 + zz
        if side == 0:
            ghosts_ref[pl.ds(base + 16, 8, stride=4), :] = eight
        else:
            ghosts_ref[pl.ds(base, 4, stride=4), :] = eight[0:4]
            ghosts_ref[pl.ds(base + 48, 4, stride=4), :] = eight[4:8]

    def store(n, first, length):
        rows = pl.ds(first, length)
        stores.append(pltpu.make_async_copy(ghosts_ref.at[rows], ghosts_hbm.at[rows], store_sem.at[n]))
        stores[-1].start()

    for load in loads:
        load.wait()
    stores = []
    for slot in range(2):
        for side in range(2):
            for zz in range(4):
                turned = got_ref[whole(side, zz, slot)].T
                for i in range(16):
                    put(turned[8 * i:8 * i + 8], i, side, zz, slot)
        store(slot, slot * 1728, 1024)
    fetch.wait()
    stores.append(pltpu.make_async_copy(kept_ref, adv_out, keep_sem.at[1]))
    stores[-1].start()
    for n in range(11):
        turned = got_ref[mixed(n)].T
        for row in range(16):
            entry, i = (16 * n + row) // 11, 16 + (16 * n + row) % 11
            put(turned[8 * row:8 * row + 8], i, entry // 8, entry % 8 // 2, entry % 2)
    for slot in range(2):
        store(2 + slot, slot * 1728 + 1024, 704)
    for copy in stores:
        copy.wait()


def per_device(populations, moment_rates, solid_bricks, owners, bricks, levels):
    hbm = pl.BlockSpec(memory_space=pl.ANY)
    padded = (3, 3, 3, CX + 2, CY + 16, NZ)
    adv, got = pl.pallas_call(
        advance,
        out_shape=(jax.ShapeDtypeStruct((27, CX, CY, NZ), F32), jax.ShapeDtypeStruct((CHUNKS, N_DEV, 128), F32)),
        in_specs=[hbm] * 6,
        out_specs=(hbm, hbm),
        scratch_shapes=[
            pltpu.VMEM((27, CX, CY, NZ), F32),
            pltpu.SMEM((27,), F32),
            pltpu.VMEM((4, 32), jnp.int32),
            pltpu.VMEM((1, 128), jnp.int32),
            pltpu.VMEM((1, 128), jnp.int32),
            pltpu.VMEM((1, 128), jnp.int32),
            pltpu.VMEM(padded, F32),
            pltpu.VMEM(padded, F32),
            pltpu.VMEM((27, CX, CY, NZ), F32),
            pltpu.VMEM((CY + 8, NZ), F32),
            pltpu.VMEM((1024, 1024), BF16),
            pltpu.VMEM((2, 2, 4, 256, NZ), F32),
            pltpu.VMEM((256, 1024), BF16),
            pltpu.VMEM((256, 1024), BF16),
            pltpu.VMEM((CHUNKS, N_DEV, 128), F32),
            pltpu.SemaphoreType.DMA((CX + 5,)),
            pltpu.SemaphoreType.DMA((2, 8)),
            pltpu.SemaphoreType.DMA((2, 8)),
            pltpu.SemaphoreType.DMA,
            pltpu.SemaphoreType.DMA((4,)),
            pltpu.SemaphoreType.DMA((4,)),
        ],
        compiler_params=pltpu.CompilerParams(collective_id=0, has_side_effects=True, vmem_limit_bytes=60 << 20),
        name="advance",
    )(populations, moment_rates, solid_bricks.reshape(4, 32), owners.reshape(1, 128), bricks.reshape(1, 128), levels.reshape(1, 128))
    adv, ghosts = pl.pallas_call(
        arrange,
        out_shape=(jax.ShapeDtypeStruct((27, CX, CY, NZ), F32), jax.ShapeDtypeStruct((2 * 1728, N_DEV), F32)),
        in_specs=[hbm, hbm],
        out_specs=(hbm, hbm),
        scratch_shapes=[
            pltpu.VMEM((CHUNKS, N_DEV, 128), F32),
            pltpu.VMEM((2 * 1728, N_DEV), F32),
            pltpu.VMEM((27, CX, CY, NZ), F32),
            pltpu.SemaphoreType.DMA((2,)),
            pltpu.SemaphoreType.DMA((4,)),
            pltpu.SemaphoreType.DMA((4,)),
        ],
        compiler_params=pltpu.CompilerParams(vmem_limit_bytes=60 << 20),
        name="arrange",
    )(adv, got)
    return adv, ghosts.reshape(2, 1728, N_DEV).transpose(2, 0, 1)


def solution(mesh):
    return jax.shard_map(
        per_device,
        mesh=mesh,
        in_specs=(
            P(None, "stream", "depth", None),
            P(),
            P("stream", "depth", None),
            P(("stream", "depth"), None),
            P(("stream", "depth")),
            P(("stream", "depth")),
        ),
        out_specs=(P(None, "stream", "depth", None), P(("stream", "depth"), None, None)),
        check_vma=False,
    )
```

```python
import itertools
import random

import jax
import jax.numpy as jnp
import numpy as np
from jax import lax
from jax.experimental import pallas as pl
from jax.experimental.pallas import tpu as pltpu
from jax.sharding import PartitionSpec as P

LOGICAL = pl.DeviceIdType.LOGICAL
F32 = jnp.float32
BF16 = jnp.bfloat16

N_STREAM = 32
N_DEPTH = 4
N_DEV = N_STREAM * N_DEPTH
CX = 4
CY = 16
NZ = 128
TOP = 8
CHUNKS = 27

line = np.array([1.0 / 6.0, 2.0 / 3.0, 1.0 / 6.0])
power_table = np.array([[1.0, 1.0, 1.0], [-1.0, 0.0, 1.0], [1.0, 0.0, 1.0]])
VELOCITIES = list(itertools.product(range(3), repeat=3))


def equilibrium_terms():
    rows = []
    for a, b, c in VELOCITIES:
        w = line[a] * line[b] * line[c]
        x, y, z = a - 1.0, b - 1.0, c - 1.0
        square = [4.5 * x * x - 1.5, 4.5 * y * y - 1.5, 4.5 * z * z - 1.5]
        rows.append([w * t for t in [1.0, 3 * x, 3 * y, 3 * z] + square + [9 * x * y, 9 * x * z, 9 * y * z]])
    rows = np.array(rows)
    moments = np.kron(np.kron(power_table, power_table), power_table) @ rows
    return rows, np.where(np.abs(moments) < 1e-12, 0.0, moments)


GEQ_TERMS, MOMENT_TERMS = equilibrium_terms()


def combine(coefficients, basis):
    groups = {}
    for value, term in zip(coefficients, basis):
        if value != 0.0:
            groups.setdefault(round(float(value), 12), []).append(term)
    total = None
    for value, terms in groups.items():
        part = terms[0]
        for term in terms[1:]:
            part = part + term
        if value != 1.0:
            part = part * np.float32(value)
        total = part if total is None else total + part
    return total


def along(values, step):
    for axis in (2, 1, 0):
        out = {}
        for key in values:
            if key[axis] == 0:
                keys = [key[:axis] + (j,) + key[axis + 1:] for j in range(3)]
                for k, v in zip(keys, step(*[values[k] for k in keys])):
                    out[k] = v
        values = out
    return values


def to_moments(f0, f1, f2):
    ends = f0 + f2
    return ends + f1, f2 - f0, ends


def from_moments(m0, h1, h2):
    return h2 - h1, m0 - (h2 + h2), h2 + h1


def collide(f, solid, rate):
    moments = along(dict(zip(VELOCITIES, f)), to_moments)
    rho, jx, jy, jz = moments[0, 0, 0], moments[1, 0, 0], moments[0, 1, 0], moments[0, 0, 1]
    inverse = 1.0 / rho
    ux, uy, uz = jx * inverse, jy * inverse, jz * inverse
    basis = [rho, rho * ux, rho * uy, rho * uz, jx * ux, jy * uy, jz * uz, jx * uy, jx * uz, jy * uz]
    change = {}
    for k, key in enumerate(VELOCITIES):
        balance = combine(MOMENT_TERMS[k], basis)
        excess = moments[key] if balance is None else moments[key] - balance
        change[key] = excess * rate(k)
    change = along(change, from_moments)
    return [jnp.where(solid, f[26 - i], f[i] - change[key]) for i, key in enumerate(VELOCITIES)]


def rescaled(f, factors):
    rho = f[0]
    for value in f[1:]:
        rho = rho + value
    speeds = []
    for axis in range(3):
        up = [f[i] for i, v in enumerate(VELOCITIES) if v[axis] == 2]
        down = [f[i] for i, v in enumerate(VELOCITIES) if v[axis] == 0]
        total = up[0]
        for value in up[1:]:
            total = total + value
        for value in down:
            total = total - value
        speeds.append(total)
    inverse = 1.0 / rho
    jx, jy, jz = speeds
    ux, uy, uz = jx * inverse, jy * inverse, jz * inverse
    xx, yy, zz = jx * ux, jy * uy, jz * uz
    still = rho - 1.5 * (xx + yy + zz)
    out = [[None] * 27 for _ in factors]
    for i in range(14):
        a, b, c = (v - 1 for v in VELOCITIES[i])
        weight = np.float32(np.prod([line[v] for v in VELOCITIES[i]]))
        even, odd = still, None
        flow = None
        for sign, j, u in ((a, jx, ux), (b, jy, uy), (c, jz, uz)):
            if sign:
                flow = ((j, u) if sign > 0 else (-j, -u)) if flow is None else (
                    (flow[0] + j, flow[1] + u) if sign > 0 else (flow[0] - j, flow[1] - u))
        if flow is not None:
            even = still + 4.5 * (flow[0] * flow[1])
            odd = (3.0 * weight) * flow[0]
        even = even * weight
        for n, balance in ((i, even if odd is None else even + odd), (26 - i, even if odd is None else even - odd)):
            off = f[n] - balance
            for level, factor in enumerate(factors):
                out[level][n] = balance + factor * off
    return out


def hops(k):
    return sum((0, 1, 2, 1)[part] for part in ((k >> 2) & 3, (k >> 4) & 3, (k >> 1) & 1 | (k >> 5) & 2))


def others():
    every = list(range(1, N_DEV))
    random.Random(1).shuffle(every)
    return every


def advance(pop_hbm, rates_hbm, solid_hbm, owners_hbm, bricks_hbm, levels_hbm, adv_ref, got_ref,
            pop_ref, rates_ref, solid_ref, owners_ref, bricks_ref, levels_ref,
            coll0, coll1, final, mask_ref, pick, fine, table_hi, table_lo, out_buf,
            load_sem, halo_send, halo_recv, adv_sem, far_send, far_recv, joined):
    loads = [pltpu.make_async_copy(pop_hbm.at[:, layer], pop_ref.at[:, layer], load_sem.at[layer]) for layer in range(CX)]
    small = [(rates_hbm, rates_ref), (solid_hbm, solid_ref), (owners_hbm, owners_ref), (bricks_hbm, bricks_ref), (levels_hbm, levels_ref)]
    loads += [pltpu.make_async_copy(a, b, load_sem.at[CX + i]) for i, (a, b) in enumerate(small)]
    for n in (4, 5, 0, 3, 1, 2, 6, 7, 8):
        loads[n].start()
    s, p = lax.axis_index("stream"), lax.axis_index("depth")
    me = s * N_DEPTH + p
    flips = [(1 << b) * (1 - 2 * ((me // (1 << b)) % 2)) for b in range(7)]
    low, high = [0], [me]
    for b in range(3):
        low = low + [t + flips[b] for t in low]
    for b in range(3, 7):
        high = high + [t + flips[b] for t in high]

    def place(k):
        return high[k >> 3] + low[k & 7]

    def beside(dx, dy):
        return ((s + dx + N_STREAM) % N_STREAM) * N_DEPTH + (p + dy + N_DEPTH) % N_DEPTH

    barrier = pltpu.get_barrier_semaphore()
    for n in SIDE_X:
        pl.semaphore_signal(barrier, inc=1, device_id=beside(*HALO[n]), device_id_type=LOGICAL)
    for k in sorted(PLANE + COLUMN, key=lambda k: -hops(k)):
        pl.semaphore_signal(barrier, inc=1, device_id=place(k), device_id_type=LOGICAL)

    for n in (4, 5):
        loads[n].wait()
    spread = (lax.broadcasted_iota(jnp.int32, (32, NZ), 1) // 4 == lax.broadcasted_iota(jnp.int32, (32, NZ), 0)).astype(BF16)
    by_row = jnp.dot(solid_ref[...].astype(F32).astype(BF16), spread, preferred_element_type=F32)
    row = lax.broadcasted_iota(jnp.int32, (CY, NZ), 0) // 4
    mask = jnp.zeros((CY, NZ), F32)
    for b in range(CY // 4):
        mask = jnp.where(row == b, jnp.broadcast_to(by_row[b:b + 1, :], (CY, NZ)), mask)
    mask_ref[pl.ds(0, CY), :] = mask

    def rate(k):
        halves = sum(1 for v in VELOCITIES[k] if v > 0)
        return rates_ref[k] * np.float32(0.5 ** halves)

    def moved(source, i, layer, half):
        a, b, c = VELOCITIES[i]
        value = source[a, b, c, layer + 2 - a, pl.ds(TOP + 8 * half + 1 - b, 8), :]
        return value if c == 1 else pltpu.roll(value, (c - 1) % NZ, 1)

    def collide_layer(layer, source, target):
        for half in range(2):
            rows = pl.ds(8 * half, 8)
            if source is None:
                f = [pop_ref[i, layer, rows, :] for i in range(27)]
            else:
                f = [moved(source, i, layer, half) for i in range(27)]
            for v, value in zip(VELOCITIES, collide(f, mask_ref[rows, :] > 0.5, rate)):
                target[v[0], v[1], v[2], layer + 1, pl.ds(TOP + 8 * half, 8), :] = value

    def halo(step, n):
        dx, dy = HALO[n]
        buf, deep = (coll0, 2) if step == 0 else (coll1, 1)
        sx, lx = {1: (CX, 0), -1: (1, CX + 1), 0: (pl.ds(1, CX),) * 2}[dx]
        sy, ly = {1: (TOP + CY - deep, TOP - deep), -1: (TOP, TOP + CY), 0: (TOP,) * 2}[dy]
        rows = CY if dy == 0 else deep
        a = {1: pl.ds(2, 1), -1: pl.ds(0, 1), 0: slice(None)}[dx]
        b = {1: pl.ds(3 - deep, deep), -1: pl.ds(0, deep), 0: slice(None)}[dy]
        return pltpu.make_async_remote_copy(
            buf.at[a, b, :, sx, pl.ds(sy, rows)], buf.at[a, b, :, lx, pl.ds(ly, rows)],
            halo_send.at[step, n], halo_recv.at[step, n], device_id=beside(dx, dy), device_id_type=LOGICAL)

    def mask_row(n):
        dy = HALO[n][1]
        return pltpu.make_async_remote_copy(
            mask_ref.at[pl.ds(CY - 1 if dy > 0 else 0, 1)], mask_ref.at[pl.ds(CY if dy > 0 else CY + 1, 1)],
            halo_send.at[1, n], halo_recv.at[1, n], device_id=beside(0, dy), device_id_type=LOGICAL)

    def collide_edges():
        f = []
        for a, b, c in VELOCITIES:
            value = jnp.concatenate(
                [coll0[a, b, c, layer + 2 - a, pl.ds(TOP - b, 2, stride=CY + 1), :] for layer in range(CX)], axis=0)
            f.append(value if c == 1 else pltpu.roll(value, (c - 1) % NZ, 1))
        solid = jnp.concatenate([mask_ref[pl.ds(CY, 2), :]] * CX, axis=0)
        for (a, b, c), value in zip(VELOCITIES, collide(f, solid > 0.5, rate)):
            if b != 1:
                side = 0 if b == 2 else 1
                for layer in range(CX):
                    row = 2 * layer + side
                    coll1[a, b, c, layer + 1, pl.ds(TOP + CY if side else TOP - 1, 1), :] = value[row:row + 1]

    def sweep(layers, body):
        def once(t, _):
            body(layers(t))
            return 0
        lax.fori_loop(0, 2, once, 0)

    outer, inner = lambda t: 3 * t, lambda t: 1 + t

    for n in (0, 3):
        loads[n].wait()
    sweep(outer, lambda layer: collide_layer(layer, None, coll0))
    pl.semaphore_wait(barrier, len(SIDE_X) + len(PLANE) + len(COLUMN))
    for n in SIDE_X:
        halo(0, n).start()
    for k in sorted(COLUMN, key=lambda k: -hops(k)):
        pl.semaphore_signal(joined, inc=1, device_id=place(k), device_id_type=LOGICAL)
    for n in (1, 2):
        loads[n].wait()
    sweep(inner, lambda layer: collide_layer(layer, None, coll0))
    for n in SIDE_Y:
        mask_row(n).start()
        halo(0, n).start()

    for n in (6, 7, 8):
        loads[n].wait()
    owner_row = jnp.broadcast_to(owners_ref[...], (N_DEV, N_DEV))
    owner_col = owner_row.T
    sub = lax.broadcasted_iota(jnp.int32, (N_DEV, N_DEV), 0)
    lane = lax.broadcasted_iota(jnp.int32, (N_DEV, N_DEV), 1)
    rank = jnp.sum(jnp.where((owner_row == owner_col) & (sub < lane), 1.0, 0.0), axis=0, keepdims=True)
    code = (bricks_ref[...] + 128 * levels_ref[...] - 127).astype(F32)
    for slot in range(2):
        named = jnp.where((owner_row == sub) & (rank == slot), jnp.broadcast_to(code, (N_DEV, N_DEV)), 0.0)
        taken = (4.0 * jnp.sum(named, axis=1, keepdims=True) - 4.0).astype(jnp.int32)
        for part in range(8):
            number = lane + 128 * part
            for zz in range(4):
                pick[pl.ds((zz * 2 + slot) * 128, 128), pl.ds(part * 128, 128)] = jnp.where(
                    number == taken + zz, 1.0, 0.0).astype(BF16)
    fine[:, :, :, pl.ds(216, 40), :] = jnp.zeros((2, 2, 4, 40, NZ), F32)

    for n in SIDE_Y:
        mask_row(n).wait_recv()
        halo(0, n).wait_recv()
    sweep(inner, lambda layer: collide_layer(layer, coll0, coll1))
    for n in SIDE_X:
        halo(0, n).wait_recv()
    sweep(outer, lambda layer: collide_layer(layer, coll0, coll1))
    for n in SIDE_X:
        halo(1, n).start()
    collide_edges()

    tau = 1.0 / jnp.full((8, NZ), rates_ref[12], F32)
    factors = [(0.5 + h * (tau - 0.5)) / (h * tau) for h in (2.0, 4.0)]

    def finish(layer, side, which):
        for half in range(2):
            f = [moved(coll1, i, layer, half) for i in range(27)]
            for i in range(27):
                final[i, layer, pl.ds(8 * half, 8), :] = f[i]
            for level, values in enumerate(rescaled(f, factors)):
                for i in range(27):
                    for quarter in range(2):
                        fine[side, level, 2 * half + quarter, pl.ds(i * 8 + which * 4, 4), :] = values[i][4 * quarter:4 * quarter + 4]

    lanes = lax.broadcasted_iota(jnp.int32, (N_DEV, 128), 1)
    dims = (((1,), (1,)), ((), ()))

    def send(part):
        for k in FAR:
            to = place(k)
            pltpu.make_async_remote_copy(
                out_buf.at[PARTS[part], to], got_ref.at[PARTS[part], me],
                far_send.at[part], far_recv.at[part], device_id=to, device_id_type=LOGICAL).start()
        pltpu.make_async_copy(out_buf.at[PARTS[part], me], got_ref.at[PARTS[part], me], far_recv.at[part]).start()

    def hand_over(side):
        for level in range(2):
            for b in range(4):
                value = fine[side, level, b]
                top = value.astype(BF16)
                columns = pl.ds((level * 4 + b) * NZ, NZ)
                table_hi[:, columns] = top
                table_lo[:, columns] = (value - top.astype(F32)).astype(BF16)
        for pair in range(2):
            part = 2 * side + pair
            for zz in (2 * pair, 2 * pair + 1):
                chosen = pick[pl.ds(zz * 256, 256), :]
                got = lax.dot_general(chosen, table_hi[...], dims, preferred_element_type=F32)
                got = got + lax.dot_general(chosen, table_lo[...], dims, preferred_element_type=F32)
                for slot in range(2):
                    value = got[128 * slot:128 * slot + 128]
                    out_buf[whole(side, zz, slot)] = value[:, 0:128]
                    place_at = 88 * (side * 8 + zz * 2 + slot)
                    chunk, start = place_at // 128, place_at % 128
                    turned = value[:, 128:256]
                    if start:
                        turned = pltpu.roll(turned, start, 1)
                        out_buf[mixed(chunk)] = jnp.where(lanes < start, out_buf[mixed(chunk)], turned)
                    else:
                        out_buf[mixed(chunk)] = turned
                    if start + 88 > 128:
                        out_buf[mixed(chunk + 1)] = turned
            send(part)

    finish(1, 0, 0)
    finish(2, 0, 1)
    pl.semaphore_wait(joined, len(COLUMN))
    hand_over(0)
    for n in SIDE_X:
        halo(1, n).wait_recv()
    finish(0, 1, 0)
    finish(3, 1, 1)
    keep = pltpu.make_async_copy(final, adv_ref, adv_sem)
    keep.start()
    hand_over(1)

    for n in SIDE_X:
        halo(0, n).wait_send()
        halo(1, n).wait_send()
    for n in SIDE_Y:
        halo(0, n).wait_send()
        mask_row(n).wait_send()
    keep.wait()
    for part in range(4):
        pltpu.make_async_copy(out_buf.at[PARTS[part]], got_ref.at[PARTS[part]], far_recv.at[part]).wait()
        rest = pl.ds(0, N_DEV - 1)
        pltpu.make_async_copy(out_buf.at[PARTS[part], rest], got_ref.at[PARTS[part], rest], far_send.at[part]).wait()


FAR = others()
PLANE = [k << 2 for k in range(1, 16)]
COLUMN = [k for k in range(1, N_DEV) if not k & 60]
HALO = [(1, 0), (-1, 0), (1, 1), (1, -1), (-1, 1), (-1, -1), (0, 1), (0, -1)]
SIDE_X = [0, 1, 2, 3, 4, 5]
SIDE_Y = [6, 7]
FIRST = [0, 6, 13, 20, CHUNKS]
PARTS = [pl.ds(a, b - a) for a, b in zip(FIRST, FIRST[1:])]


def whole(side, zz, slot):
    return FIRST[2 * side + zz // 2] + zz % 2 * 2 + slot


def mixed(n):
    return ([4, 5] + [10, 11, 12] + [17, 18, 19] + [24, 25, 26])[n]


def arrange(adv_ref, got_hbm, adv_out, ghosts_hbm, got_ref, ghosts_ref, kept_ref, keep_sem, load_sem, store_sem):
    loads = [pltpu.make_async_copy(got_hbm.at[rows], got_ref.at[rows], load_sem.at[part]) for part, rows in enumerate(PARTS)]
    for load in loads:
        load.start()
    fetch = pltpu.make_async_copy(adv_ref, kept_ref, keep_sem.at[0])
    fetch.start()

    def put(eight, i, side, zz, slot):
        base = slot * 1728 + i * 64 + zz
        if side == 0:
            ghosts_ref[pl.ds(base + 16, 8, stride=4), :] = eight
        else:
            ghosts_ref[pl.ds(base, 4, stride=4), :] = eight[0:4]
            ghosts_ref[pl.ds(base + 48, 4, stride=4), :] = eight[4:8]

    def store(n, first, length):
        rows = pl.ds(first, length)
        stores.append(pltpu.make_async_copy(ghosts_ref.at[rows], ghosts_hbm.at[rows], store_sem.at[n]))
        stores[-1].start()

    for load in loads:
        load.wait()
    stores = []
    for slot in range(2):
        for side in range(2):
            for zz in range(4):
                turned = got_ref[whole(side, zz, slot)].T
                for i in range(16):
                    put(turned[8 * i:8 * i + 8], i, side, zz, slot)
        store(slot, slot * 1728, 1024)
    fetch.wait()
    stores.append(pltpu.make_async_copy(kept_ref, adv_out, keep_sem.at[1]))
    stores[-1].start()
    for n in range(11):
        turned = got_ref[mixed(n)].T
        for row in range(16):
            entry, i = (16 * n + row) // 11, 16 + (16 * n + row) % 11
            put(turned[8 * row:8 * row + 8], i, entry // 8, entry % 8 // 2, entry % 2)
    for slot in range(2):
        store(2 + slot, slot * 1728 + 1024, 704)
    for copy in stores:
        copy.wait()


def per_device(populations, moment_rates, solid_bricks, owners, bricks, levels):
    hbm = pl.BlockSpec(memory_space=pl.ANY)
    padded = (3, 3, 3, CX + 2, CY + 16, NZ)
    adv, got = pl.pallas_call(
        advance,
        out_shape=(jax.ShapeDtypeStruct((27, CX, CY, NZ), F32), jax.ShapeDtypeStruct((CHUNKS, N_DEV, 128), F32)),
        in_specs=[hbm] * 6,
        out_specs=(hbm, hbm),
        scratch_shapes=[
            pltpu.VMEM((27, CX, CY, NZ), F32),
            pltpu.SMEM((27,), F32),
            pltpu.VMEM((4, 32), jnp.int32),
            pltpu.VMEM((1, 128), jnp.int32),
            pltpu.VMEM((1, 128), jnp.int32),
            pltpu.VMEM((1, 128), jnp.int32),
            pltpu.VMEM(padded, F32),
            pltpu.VMEM(padded, F32),
            pltpu.VMEM((27, CX, CY, NZ), F32),
            pltpu.VMEM((CY + 8, NZ), F32),
            pltpu.VMEM((1024, 1024), BF16),
            pltpu.VMEM((2, 2, 4, 256, NZ), F32),
            pltpu.VMEM((256, 1024), BF16),
            pltpu.VMEM((256, 1024), BF16),
            pltpu.VMEM((CHUNKS, N_DEV, 128), F32),
            pltpu.SemaphoreType.DMA((CX + 5,)),
            pltpu.SemaphoreType.DMA((2, 8)),
            pltpu.SemaphoreType.DMA((2, 8)),
            pltpu.SemaphoreType.DMA,
            pltpu.SemaphoreType.DMA((4,)),
            pltpu.SemaphoreType.DMA((4,)),
            pltpu.SemaphoreType.REGULAR,
        ],
        compiler_params=pltpu.CompilerParams(collective_id=0, has_side_effects=True, vmem_limit_bytes=60 << 20),
        name="advance",
    )(populations, moment_rates, solid_bricks.reshape(4, 32), owners.reshape(1, 128), bricks.reshape(1, 128), levels.reshape(1, 128))
    adv, ghosts = pl.pallas_call(
        arrange,
        out_shape=(jax.ShapeDtypeStruct((27, CX, CY, NZ), F32), jax.ShapeDtypeStruct((2 * 1728, N_DEV), F32)),
        in_specs=[hbm, hbm],
        out_specs=(hbm, hbm),
        scratch_shapes=[
            pltpu.VMEM((CHUNKS, N_DEV, 128), F32),
            pltpu.VMEM((2 * 1728, N_DEV), F32),
            pltpu.VMEM((27, CX, CY, NZ), F32),
            pltpu.SemaphoreType.DMA((2,)),
            pltpu.SemaphoreType.DMA((4,)),
            pltpu.SemaphoreType.DMA((4,)),
        ],
        compiler_params=pltpu.CompilerParams(vmem_limit_bytes=60 << 20),
        name="arrange",
    )(adv, got)
    return adv, ghosts.reshape(2, 1728, N_DEV).transpose(2, 0, 1)


def solution(mesh):
    return jax.shard_map(
        per_device,
        mesh=mesh,
        in_specs=(
            P(None, "stream", "depth", None),
            P(),
            P("stream", "depth", None),
            P(("stream", "depth"), None),
            P(("stream", "depth")),
            P(("stream", "depth")),
        ),
        out_specs=(P(None, "stream", "depth", None), P(("stream", "depth"), None, None)),
        check_vma=False,
    )
```

```python
import itertools
import random

import jax
import jax.numpy as jnp
import numpy as np
from jax import lax
from jax.experimental import pallas as pl
from jax.experimental.pallas import tpu as pltpu
from jax.sharding import PartitionSpec as P

LOGICAL = pl.DeviceIdType.LOGICAL
F32 = jnp.float32
BF16 = jnp.bfloat16

N_STREAM = 32
N_DEPTH = 4
N_DEV = N_STREAM * N_DEPTH
CX = 4
CY = 16
NZ = 128
TOP = 8
CHUNKS = 27

line = np.array([1.0 / 6.0, 2.0 / 3.0, 1.0 / 6.0])
power_table = np.array([[1.0, 1.0, 1.0], [-1.0, 0.0, 1.0], [1.0, 0.0, 1.0]])
VELOCITIES = list(itertools.product(range(3), repeat=3))


def equilibrium_terms():
    rows = []
    for a, b, c in VELOCITIES:
        w = line[a] * line[b] * line[c]
        x, y, z = a - 1.0, b - 1.0, c - 1.0
        square = [4.5 * x * x - 1.5, 4.5 * y * y - 1.5, 4.5 * z * z - 1.5]
        rows.append([w * t for t in [1.0, 3 * x, 3 * y, 3 * z] + square + [9 * x * y, 9 * x * z, 9 * y * z]])
    rows = np.array(rows)
    moments = np.kron(np.kron(power_table, power_table), power_table) @ rows
    return rows, np.where(np.abs(moments) < 1e-12, 0.0, moments)


GEQ_TERMS, MOMENT_TERMS = equilibrium_terms()


def combine(coefficients, basis):
    groups = {}
    for value, term in zip(coefficients, basis):
        if value != 0.0:
            groups.setdefault(round(float(value), 12), []).append(term)
    total = None
    for value, terms in groups.items():
        part = terms[0]
        for term in terms[1:]:
            part = part + term
        if value != 1.0:
            part = part * np.float32(value)
        total = part if total is None else total + part
    return total


def along(values, step):
    for axis in (2, 1, 0):
        out = {}
        for key in values:
            if key[axis] == 0:
                keys = [key[:axis] + (j,) + key[axis + 1:] for j in range(3)]
                for k, v in zip(keys, step(*[values[k] for k in keys])):
                    out[k] = v
        values = out
    return values


def to_moments(f0, f1, f2):
    ends = f0 + f2
    return ends + f1, f2 - f0, ends


def from_moments(m0, h1, h2):
    return h2 - h1, m0 - (h2 + h2), h2 + h1


def collide(f, solid, rate):
    moments = along(dict(zip(VELOCITIES, f)), to_moments)
    rho, jx, jy, jz = moments[0, 0, 0], moments[1, 0, 0], moments[0, 1, 0], moments[0, 0, 1]
    inverse = 1.0 / rho
    ux, uy, uz = jx * inverse, jy * inverse, jz * inverse
    basis = [rho, rho * ux, rho * uy, rho * uz, jx * ux, jy * uy, jz * uz, jx * uy, jx * uz, jy * uz]
    change = {}
    for k, key in enumerate(VELOCITIES):
        balance = combine(MOMENT_TERMS[k], basis)
        excess = moments[key] if balance is None else moments[key] - balance
        change[key] = excess * rate(k)
    change = along(change, from_moments)
    return [jnp.where(solid, f[26 - i], f[i] - change[key]) for i, key in enumerate(VELOCITIES)]


def rescaled(f, factors):
    rho = f[0]
    for value in f[1:]:
        rho = rho + value
    speeds = []
    for axis in range(3):
        up = [f[i] for i, v in enumerate(VELOCITIES) if v[axis] == 2]
        down = [f[i] for i, v in enumerate(VELOCITIES) if v[axis] == 0]
        total = up[0]
        for value in up[1:]:
            total = total + value
        for value in down:
            total = total - value
        speeds.append(total)
    inverse = 1.0 / rho
    jx, jy, jz = speeds
    ux, uy, uz = jx * inverse, jy * inverse, jz * inverse
    xx, yy, zz = jx * ux, jy * uy, jz * uz
    still = rho - 1.5 * (xx + yy + zz)
    out = [[None] * 27 for _ in factors]
    for i in range(14):
        a, b, c = (v - 1 for v in VELOCITIES[i])
        weight = np.float32(np.prod([line[v] for v in VELOCITIES[i]]))
        even, odd = still, None
        flow = None
        for sign, j, u in ((a, jx, ux), (b, jy, uy), (c, jz, uz)):
            if sign:
                flow = ((j, u) if sign > 0 else (-j, -u)) if flow is None else (
                    (flow[0] + j, flow[1] + u) if sign > 0 else (flow[0] - j, flow[1] - u))
        if flow is not None:
            even = still + 4.5 * (flow[0] * flow[1])
            odd = (3.0 * weight) * flow[0]
        even = even * weight
        for n, balance in ((i, even if odd is None else even + odd), (26 - i, even if odd is None else even - odd)):
            off = f[n] - balance
            for level, factor in enumerate(factors):
                out[level][n] = balance + factor * off
    return out


def hops(k):
    return sum((0, 1, 2, 1)[part] for part in ((k >> 2) & 3, (k >> 4) & 3, (k >> 1) & 1 | (k >> 5) & 2))


def others():
    every = list(range(1, N_DEV))
    random.Random(1).shuffle(every)
    every.sort(key=lambda k: -hops(k))
    return every


def advance(pop_hbm, rates_hbm, solid_hbm, owners_hbm, bricks_hbm, levels_hbm, adv_ref, got_ref,
            pop_ref, rates_ref, solid_ref, owners_ref, bricks_ref, levels_ref,
            coll0, coll1, final, mask_ref, pick, fine, table_hi, table_lo, out_buf,
            load_sem, halo_send, halo_recv, adv_sem, far_send, far_recv, joined):
    loads = [pltpu.make_async_copy(pop_hbm.at[:, layer], pop_ref.at[:, layer], load_sem.at[layer]) for layer in range(CX)]
    small = [(rates_hbm, rates_ref), (solid_hbm, solid_ref), (owners_hbm, owners_ref), (bricks_hbm, bricks_ref), (levels_hbm, levels_ref)]
    loads += [pltpu.make_async_copy(a, b, load_sem.at[CX + i]) for i, (a, b) in enumerate(small)]
    for n in (4, 5, 0, 3, 1, 2, 6, 7, 8):
        loads[n].start()
    s, p = lax.axis_index("stream"), lax.axis_index("depth")
    me = s * N_DEPTH + p
    flips = [(1 << b) * (1 - 2 * ((me // (1 << b)) % 2)) for b in range(7)]
    low, high = [0], [me]
    for b in range(3):
        low = low + [t + flips[b] for t in low]
    for b in range(3, 7):
        high = high + [t + flips[b] for t in high]

    def place(k):
        return high[k >> 3] + low[k & 7]

    def beside(dx, dy):
        return ((s + dx + N_STREAM) % N_STREAM) * N_DEPTH + (p + dy + N_DEPTH) % N_DEPTH

    barrier = pltpu.get_barrier_semaphore()
    for n in SIDE_X:
        pl.semaphore_signal(barrier, inc=1, device_id=beside(*HALO[n]), device_id_type=LOGICAL)
    for k in sorted(PLANE + COLUMN, key=lambda k: -hops(k)):
        pl.semaphore_signal(barrier, inc=1, device_id=place(k), device_id_type=LOGICAL)

    for n in (4, 5):
        loads[n].wait()
    spread = (lax.broadcasted_iota(jnp.int32, (32, NZ), 1) // 4 == lax.broadcasted_iota(jnp.int32, (32, NZ), 0)).astype(BF16)
    by_row = jnp.dot(solid_ref[...].astype(F32).astype(BF16), spread, preferred_element_type=F32)
    row = lax.broadcasted_iota(jnp.int32, (CY, NZ), 0) // 4
    mask = jnp.zeros((CY, NZ), F32)
    for b in range(CY // 4):
        mask = jnp.where(row == b, jnp.broadcast_to(by_row[b:b + 1, :], (CY, NZ)), mask)
    mask_ref[pl.ds(0, CY), :] = mask

    def rate(k):
        halves = sum(1 for v in VELOCITIES[k] if v > 0)
        return rates_ref[k] * np.float32(0.5 ** halves)

    def moved(source, i, layer, half):
        a, b, c = VELOCITIES[i]
        value = source[a, b, c, layer + 2 - a, pl.ds(TOP + 8 * half + 1 - b, 8), :]
        return value if c == 1 else pltpu.roll(value, (c - 1) % NZ, 1)

    def collide_layer(layer, source, target):
        for half in range(2):
            rows = pl.ds(8 * half, 8)
            if source is None:
                f = [pop_ref[i, layer, rows, :] for i in range(27)]
            else:
                f = [moved(source, i, layer, half) for i in range(27)]
            for v, value in zip(VELOCITIES, collide(f, mask_ref[rows, :] > 0.5, rate)):
                target[v[0], v[1], v[2], layer + 1, pl.ds(TOP + 8 * half, 8), :] = value

    def halo(step, n):
        dx, dy = HALO[n]
        buf, deep = (coll0, 2) if step == 0 else (coll1, 1)
        sx, lx = {1: (CX, 0), -1: (1, CX + 1), 0: (pl.ds(1, CX),) * 2}[dx]
        sy, ly = {1: (TOP + CY - deep, TOP - deep), -1: (TOP, TOP + CY), 0: (TOP,) * 2}[dy]
        rows = CY if dy == 0 else deep
        a = {1: pl.ds(2, 1), -1: pl.ds(0, 1), 0: slice(None)}[dx]
        b = {1: pl.ds(3 - deep, deep), -1: pl.ds(0, deep), 0: slice(None)}[dy]
        return pltpu.make_async_remote_copy(
            buf.at[a, b, :, sx, pl.ds(sy, rows)], buf.at[a, b, :, lx, pl.ds(ly, rows)],
            halo_send.at[step, n], halo_recv.at[step, n], device_id=beside(dx, dy), device_id_type=LOGICAL)

    def mask_row(n):
        dy = HALO[n][1]
        return pltpu.make_async_remote_copy(
            mask_ref.at[pl.ds(CY - 1 if dy > 0 else 0, 1)], mask_ref.at[pl.ds(CY if dy > 0 else CY + 1, 1)],
            halo_send.at[1, n], halo_recv.at[1, n], device_id=beside(0, dy), device_id_type=LOGICAL)

    def collide_edges():
        f = []
        for a, b, c in VELOCITIES:
            value = jnp.concatenate(
                [coll0[a, b, c, layer + 2 - a, pl.ds(TOP - b, 2, stride=CY + 1), :] for layer in range(CX)], axis=0)
            f.append(value if c == 1 else pltpu.roll(value, (c - 1) % NZ, 1))
        solid = jnp.concatenate([mask_ref[pl.ds(CY, 2), :]] * CX, axis=0)
        for (a, b, c), value in zip(VELOCITIES, collide(f, solid > 0.5, rate)):
            if b != 1:
                side = 0 if b == 2 else 1
                for layer in range(CX):
                    row = 2 * layer + side
                    coll1[a, b, c, layer + 1, pl.ds(TOP + CY if side else TOP - 1, 1), :] = value[row:row + 1]

    def sweep(layers, body):
        def once(t, _):
            body(layers(t))
            return 0
        lax.fori_loop(0, 2, once, 0)

    outer, inner = lambda t: 3 * t, lambda t: 1 + t

    for n in (0, 3):
        loads[n].wait()
    sweep(outer, lambda layer: collide_layer(layer, None, coll0))
    pl.semaphore_wait(barrier, len(SIDE_X) + len(PLANE) + len(COLUMN))
    for n in SIDE_X:
        halo(0, n).start()
    for k in sorted(COLUMN, key=lambda k: -hops(k)):
        pl.semaphore_signal(joined, inc=1, device_id=place(k), device_id_type=LOGICAL)
    for n in (1, 2):
        loads[n].wait()
    sweep(inner, lambda layer: collide_layer(layer, None, coll0))
    for n in SIDE_Y:
        mask_row(n).start()
        halo(0, n).start()

    for n in (6, 7, 8):
        loads[n].wait()
    owner_row = jnp.broadcast_to(owners_ref[...], (N_DEV, N_DEV))
    owner_col = owner_row.T
    sub = lax.broadcasted_iota(jnp.int32, (N_DEV, N_DEV), 0)
    lane = lax.broadcasted_iota(jnp.int32, (N_DEV, N_DEV), 1)
    rank = jnp.sum(jnp.where((owner_row == owner_col) & (sub < lane), 1.0, 0.0), axis=0, keepdims=True)
    code = (bricks_ref[...] + 128 * levels_ref[...] - 127).astype(F32)
    for slot in range(2):
        named = jnp.where((owner_row == sub) & (rank == slot), jnp.broadcast_to(code, (N_DEV, N_DEV)), 0.0)
        taken = (4.0 * jnp.sum(named, axis=1, keepdims=True) - 4.0).astype(jnp.int32)
        for part in range(8):
            number = lane + 128 * part
            for zz in range(4):
                pick[pl.ds((zz * 2 + slot) * 128, 128), pl.ds(part * 128, 128)] = jnp.where(
                    number == taken + zz, 1.0, 0.0).astype(BF16)
    fine[:, :, :, pl.ds(216, 40), :] = jnp.zeros((2, 2, 4, 40, NZ), F32)

    for n in SIDE_Y:
        mask_row(n).wait_recv()
        halo(0, n).wait_recv()
    sweep(inner, lambda layer: collide_layer(layer, coll0, coll1))
    for n in SIDE_X:
        halo(0, n).wait_recv()
    sweep(outer, lambda layer: collide_layer(layer, coll0, coll1))
    for n in SIDE_X:
        halo(1, n).start()
    collide_edges()

    tau = 1.0 / jnp.full((8, NZ), rates_ref[12], F32)
    factors = [(0.5 + h * (tau - 0.5)) / (h * tau) for h in (2.0, 4.0)]

    def finish(layer, side, which):
        for half in range(2):
            f = [moved(coll1, i, layer, half) for i in range(27)]
            for i in range(27):
                final[i, layer, pl.ds(8 * half, 8), :] = f[i]
            for level, values in enumerate(rescaled(f, factors)):
                for i in range(27):
                    for quarter in range(2):
                        fine[side, level, 2 * half + quarter, pl.ds(i * 8 + which * 4, 4), :] = values[i][4 * quarter:4 * quarter + 4]

    lanes = lax.broadcasted_iota(jnp.int32, (N_DEV, 128), 1)
    dims = (((1,), (1,)), ((), ()))

    def send(part):
        for k in FAR:
            to = place(k)
            pltpu.make_async_remote_copy(
                out_buf.at[PARTS[part], to], got_ref.at[PARTS[part], me],
                far_send.at[part], far_recv.at[part], device_id=to, device_id_type=LOGICAL).start()
        pltpu.make_async_copy(out_buf.at[PARTS[part], me], got_ref.at[PARTS[part], me], far_recv.at[part]).start()

    def hand_over(side):
        for level in range(2):
            for b in range(4):
                value = fine[side, level, b]
                top = value.astype(BF16)
                columns = pl.ds((level * 4 + b) * NZ, NZ)
                table_hi[:, columns] = top
                table_lo[:, columns] = (value - top.astype(F32)).astype(BF16)
        for pair in range(2):
            part = 2 * side + pair
            for zz in (2 * pair, 2 * pair + 1):
                chosen = pick[pl.ds(zz * 256, 256), :]
                got = lax.dot_general(chosen, table_hi[...], dims, preferred_element_type=F32)
                got = got + lax.dot_general(chosen, table_lo[...], dims, preferred_element_type=F32)
                for slot in range(2):
                    value = got[128 * slot:128 * slot + 128]
                    out_buf[whole(side, zz, slot)] = value[:, 0:128]
                    place_at = 88 * (side * 8 + zz * 2 + slot)
                    chunk, start = place_at // 128, place_at % 128
                    turned = value[:, 128:256]
                    if start:
                        turned = pltpu.roll(turned, start, 1)
                        out_buf[mixed(chunk)] = jnp.where(lanes < start, out_buf[mixed(chunk)], turned)
                    else:
                        out_buf[mixed(chunk)] = turned
                    if start + 88 > 128:
                        out_buf[mixed(chunk + 1)] = turned
            send(part)

    finish(1, 0, 0)
    finish(2, 0, 1)
    pl.semaphore_wait(joined, len(COLUMN))
    hand_over(0)
    for n in SIDE_X:
        halo(1, n).wait_recv()
    finish(0, 1, 0)
    finish(3, 1, 1)
    keep = pltpu.make_async_copy(final, adv_ref, adv_sem)
    keep.start()
    hand_over(1)

    for n in SIDE_X:
        halo(0, n).wait_send()
        halo(1, n).wait_send()
    for n in SIDE_Y:
        halo(0, n).wait_send()
        mask_row(n).wait_send()
    keep.wait()
    for part in range(4):
        pltpu.make_async_copy(out_buf.at[PARTS[part]], got_ref.at[PARTS[part]], far_recv.at[part]).wait()
        rest = pl.ds(0, N_DEV - 1)
        pltpu.make_async_copy(out_buf.at[PARTS[part], rest], got_ref.at[PARTS[part], rest], far_send.at[part]).wait()


FAR = others()
PLANE = [k << 2 for k in range(1, 16)]
COLUMN = [k for k in range(1, N_DEV) if not k & 60]
HALO = [(1, 0), (-1, 0), (1, 1), (1, -1), (-1, 1), (-1, -1), (0, 1), (0, -1)]
SIDE_X = [0, 1, 2, 3, 4, 5]
SIDE_Y = [6, 7]
FIRST = [0, 6, 13, 20, CHUNKS]
PARTS = [pl.ds(a, b - a) for a, b in zip(FIRST, FIRST[1:])]


def whole(side, zz, slot):
    return FIRST[2 * side + zz // 2] + zz % 2 * 2 + slot


def mixed(n):
    return ([4, 5] + [10, 11, 12] + [17, 18, 19] + [24, 25, 26])[n]


def arrange(adv_ref, got_hbm, adv_out, ghosts_hbm, got_ref, ghosts_ref, kept_ref, keep_sem, load_sem, store_sem):
    loads = [pltpu.make_async_copy(got_hbm.at[rows], got_ref.at[rows], load_sem.at[part]) for part, rows in enumerate(PARTS)]
    for load in loads:
        load.start()
    fetch = pltpu.make_async_copy(adv_ref, kept_ref, keep_sem.at[0])
    fetch.start()

    def put(eight, i, side, zz, slot):
        base = slot * 1728 + i * 64 + zz
        if side == 0:
            ghosts_ref[pl.ds(base + 16, 8, stride=4), :] = eight
        else:
            ghosts_ref[pl.ds(base, 4, stride=4), :] = eight[0:4]
            ghosts_ref[pl.ds(base + 48, 4, stride=4), :] = eight[4:8]

    def store(n, first, length):
        rows = pl.ds(first, length)
        stores.append(pltpu.make_async_copy(ghosts_ref.at[rows], ghosts_hbm.at[rows], store_sem.at[n]))
        stores[-1].start()

    for load in loads:
        load.wait()
    stores = []
    for slot in range(2):
        for side in range(2):
            for zz in range(4):
                turned = got_ref[whole(side, zz, slot)].T
                for i in range(16):
                    put(turned[8 * i:8 * i + 8], i, side, zz, slot)
        store(slot, slot * 1728, 1024)
    fetch.wait()
    stores.append(pltpu.make_async_copy(kept_ref, adv_out, keep_sem.at[1]))
    stores[-1].start()
    for n in range(11):
        turned = got_ref[mixed(n)].T
        for row in range(16):
            entry, i = (16 * n + row) // 11, 16 + (16 * n + row) % 11
            put(turned[8 * row:8 * row + 8], i, entry // 8, entry % 8 // 2, entry % 2)
    for slot in range(2):
        store(2 + slot, slot * 1728 + 1024, 704)
    for copy in stores:
        copy.wait()


def per_device(populations, moment_rates, solid_bricks, owners, bricks, levels):
    hbm = pl.BlockSpec(memory_space=pl.ANY)
    padded = (3, 3, 3, CX + 2, CY + 16, NZ)
    adv, got = pl.pallas_call(
        advance,
        out_shape=(jax.ShapeDtypeStruct((27, CX, CY, NZ), F32), jax.ShapeDtypeStruct((CHUNKS, N_DEV, 128), F32)),
        in_specs=[hbm] * 6,
        out_specs=(hbm, hbm),
        scratch_shapes=[
            pltpu.VMEM((27, CX, CY, NZ), F32),
            pltpu.SMEM((27,), F32),
            pltpu.VMEM((4, 32), jnp.int32),
            pltpu.VMEM((1, 128), jnp.int32),
            pltpu.VMEM((1, 128), jnp.int32),
            pltpu.VMEM((1, 128), jnp.int32),
            pltpu.VMEM(padded, F32),
            pltpu.VMEM(padded, F32),
            pltpu.VMEM((27, CX, CY, NZ), F32),
            pltpu.VMEM((CY + 8, NZ), F32),
            pltpu.VMEM((1024, 1024), BF16),
            pltpu.VMEM((2, 2, 4, 256, NZ), F32),
            pltpu.VMEM((256, 1024), BF16),
            pltpu.VMEM((256, 1024), BF16),
            pltpu.VMEM((CHUNKS, N_DEV, 128), F32),
            pltpu.SemaphoreType.DMA((CX + 5,)),
            pltpu.SemaphoreType.DMA((2, 8)),
            pltpu.SemaphoreType.DMA((2, 8)),
            pltpu.SemaphoreType.DMA,
            pltpu.SemaphoreType.DMA((4,)),
            pltpu.SemaphoreType.DMA((4,)),
            pltpu.SemaphoreType.REGULAR,
        ],
        compiler_params=pltpu.CompilerParams(collective_id=0, has_side_effects=True, vmem_limit_bytes=60 << 20),
        name="advance",
    )(populations, moment_rates, solid_bricks.reshape(4, 32), owners.reshape(1, 128), bricks.reshape(1, 128), levels.reshape(1, 128))
    adv, ghosts = pl.pallas_call(
        arrange,
        out_shape=(jax.ShapeDtypeStruct((27, CX, CY, NZ), F32), jax.ShapeDtypeStruct((2 * 1728, N_DEV), F32)),
        in_specs=[hbm, hbm],
        out_specs=(hbm, hbm),
        scratch_shapes=[
            pltpu.VMEM((CHUNKS, N_DEV, 128), F32),
            pltpu.VMEM((2 * 1728, N_DEV), F32),
            pltpu.VMEM((27, CX, CY, NZ), F32),
            pltpu.SemaphoreType.DMA((2,)),
            pltpu.SemaphoreType.DMA((4,)),
            pltpu.SemaphoreType.DMA((4,)),
        ],
        compiler_params=pltpu.CompilerParams(vmem_limit_bytes=60 << 20),
        name="arrange",
    )(adv, got)
    return adv, ghosts.reshape(2, 1728, N_DEV).transpose(2, 0, 1)


def solution(mesh):
    return jax.shard_map(
        per_device,
        mesh=mesh,
        in_specs=(
            P(None, "stream", "depth", None),
            P(),
            P("stream", "depth", None),
            P(("stream", "depth"), None),
            P(("stream", "depth")),
            P(("stream", "depth")),
        ),
        out_specs=(P(None, "stream", "depth", None), P(("stream", "depth"), None, None)),
        check_vma=False,
    )
```

```python
import itertools
import random

import jax
import jax.numpy as jnp
import numpy as np
from jax import lax
from jax.experimental import pallas as pl
from jax.experimental.pallas import tpu as pltpu
from jax.sharding import PartitionSpec as P

LOGICAL = pl.DeviceIdType.LOGICAL
F32 = jnp.float32
BF16 = jnp.bfloat16

N_STREAM = 32
N_DEPTH = 4
N_DEV = N_STREAM * N_DEPTH
CX = 4
CY = 16
NZ = 128
TOP = 8
CHUNKS = 27

line = np.array([1.0 / 6.0, 2.0 / 3.0, 1.0 / 6.0])
power_table = np.array([[1.0, 1.0, 1.0], [-1.0, 0.0, 1.0], [1.0, 0.0, 1.0]])
VELOCITIES = list(itertools.product(range(3), repeat=3))


def equilibrium_terms():
    rows = []
    for a, b, c in VELOCITIES:
        w = line[a] * line[b] * line[c]
        x, y, z = a - 1.0, b - 1.0, c - 1.0
        square = [4.5 * x * x - 1.5, 4.5 * y * y - 1.5, 4.5 * z * z - 1.5]
        rows.append([w * t for t in [1.0, 3 * x, 3 * y, 3 * z] + square + [9 * x * y, 9 * x * z, 9 * y * z]])
    rows = np.array(rows)
    moments = np.kron(np.kron(power_table, power_table), power_table) @ rows
    return rows, np.where(np.abs(moments) < 1e-12, 0.0, moments)


GEQ_TERMS, MOMENT_TERMS = equilibrium_terms()


def combine(coefficients, basis):
    groups = {}
    for value, term in zip(coefficients, basis):
        if value != 0.0:
            groups.setdefault(round(float(value), 12), []).append(term)
    total = None
    for value, terms in groups.items():
        part = terms[0]
        for term in terms[1:]:
            part = part + term
        if value != 1.0:
            part = part * np.float32(value)
        total = part if total is None else total + part
    return total


def along(values, step):
    for axis in (2, 1, 0):
        out = {}
        for key in values:
            if key[axis] == 0:
                keys = [key[:axis] + (j,) + key[axis + 1:] for j in range(3)]
                for k, v in zip(keys, step(*[values[k] for k in keys])):
                    out[k] = v
        values = out
    return values


def to_moments(f0, f1, f2):
    ends = f0 + f2
    return ends + f1, f2 - f0, ends


def from_moments(m0, h1, h2):
    return h2 - h1, m0 - (h2 + h2), h2 + h1


def collide(f, solid, rate):
    moments = along(dict(zip(VELOCITIES, f)), to_moments)
    rho, jx, jy, jz = moments[0, 0, 0], moments[1, 0, 0], moments[0, 1, 0], moments[0, 0, 1]
    inverse = 1.0 / rho
    ux, uy, uz = jx * inverse, jy * inverse, jz * inverse
    basis = [rho, rho * ux, rho * uy, rho * uz, jx * ux, jy * uy, jz * uz, jx * uy, jx * uz, jy * uz]
    change = {}
    for k, key in enumerate(VELOCITIES):
        balance = combine(MOMENT_TERMS[k], basis)
        excess = moments[key] if balance is None else moments[key] - balance
        change[key] = excess * rate(k)
    change = along(change, from_moments)
    return [jnp.where(solid, f[26 - i], f[i] - change[key]) for i, key in enumerate(VELOCITIES)]


def rescaled(f, factors):
    rho = f[0]
    for value in f[1:]:
        rho = rho + value
    speeds = []
    for axis in range(3):
        up = [f[i] for i, v in enumerate(VELOCITIES) if v[axis] == 2]
        down = [f[i] for i, v in enumerate(VELOCITIES) if v[axis] == 0]
        total = up[0]
        for value in up[1:]:
            total = total + value
        for value in down:
            total = total - value
        speeds.append(total)
    inverse = 1.0 / rho
    jx, jy, jz = speeds
    ux, uy, uz = jx * inverse, jy * inverse, jz * inverse
    xx, yy, zz = jx * ux, jy * uy, jz * uz
    still = rho - 1.5 * (xx + yy + zz)
    out = [[None] * 27 for _ in factors]
    for i in range(14):
        a, b, c = (v - 1 for v in VELOCITIES[i])
        weight = np.float32(np.prod([line[v] for v in VELOCITIES[i]]))
        even, odd = still, None
        flow = None
        for sign, j, u in ((a, jx, ux), (b, jy, uy), (c, jz, uz)):
            if sign:
                flow = ((j, u) if sign > 0 else (-j, -u)) if flow is None else (
                    (flow[0] + j, flow[1] + u) if sign > 0 else (flow[0] - j, flow[1] - u))
        if flow is not None:
            even = still + 4.5 * (flow[0] * flow[1])
            odd = (3.0 * weight) * flow[0]
        even = even * weight
        for n, balance in ((i, even if odd is None else even + odd), (26 - i, even if odd is None else even - odd)):
            off = f[n] - balance
            for level, factor in enumerate(factors):
                out[level][n] = balance + factor * off
    return out


def hops(k):
    return sum((0, 1, 2, 1)[part] for part in ((k >> 2) & 3, (k >> 4) & 3, (k >> 1) & 1 | (k >> 5) & 2))


def others():
    every = list(range(1, N_DEV))
    random.Random(1).shuffle(every)
    every.sort(key=lambda k: -hops(k))
    return every


def advance(pop_hbm, rates_hbm, solid_hbm, owners_hbm, bricks_hbm, levels_hbm, adv_ref, got_ref,
            pop_ref, rates_ref, solid_ref, owners_ref, bricks_ref, levels_ref,
            coll0, coll1, final, mask_ref, pick, fine, table_hi, table_lo, out_buf,
            load_sem, halo_send, halo_recv, adv_sem, far_send, far_recv, joined):
    loads = [pltpu.make_async_copy(pop_hbm.at[:, layer], pop_ref.at[:, layer], load_sem.at[layer]) for layer in range(CX)]
    small = [(rates_hbm, rates_ref), (solid_hbm, solid_ref), (owners_hbm, owners_ref), (bricks_hbm, bricks_ref), (levels_hbm, levels_ref)]
    loads += [pltpu.make_async_copy(a, b, load_sem.at[CX + i]) for i, (a, b) in enumerate(small)]
    for n in (4, 5, 0, 3, 1, 2, 6, 7, 8):
        loads[n].start()
    s, p = lax.axis_index("stream"), lax.axis_index("depth")
    me = s * N_DEPTH + p
    flips = [(1 << b) * (1 - 2 * ((me // (1 << b)) % 2)) for b in range(7)]
    low, high = [0], [me]
    for b in range(3):
        low = low + [t + flips[b] for t in low]
    for b in range(3, 7):
        high = high + [t + flips[b] for t in high]

    def place(k):
        return high[k >> 3] + low[k & 7]

    def beside(dx, dy):
        return ((s + dx + N_STREAM) % N_STREAM) * N_DEPTH + (p + dy + N_DEPTH) % N_DEPTH

    barrier = pltpu.get_barrier_semaphore()
    for n in SIDE_X:
        pl.semaphore_signal(barrier, inc=1, device_id=beside(*HALO[n]), device_id_type=LOGICAL)
    for k in sorted(PLANE + COLUMN, key=lambda k: -hops(k)):
        pl.semaphore_signal(barrier, inc=1, device_id=place(k), device_id_type=LOGICAL)

    for n in (4, 5):
        loads[n].wait()
    spread = (lax.broadcasted_iota(jnp.int32, (32, NZ), 1) // 4 == lax.broadcasted_iota(jnp.int32, (32, NZ), 0)).astype(BF16)
    by_row = jnp.dot(solid_ref[...].astype(F32).astype(BF16), spread, preferred_element_type=F32)
    row = lax.broadcasted_iota(jnp.int32, (CY, NZ), 0) // 4
    mask = jnp.zeros((CY, NZ), F32)
    for b in range(CY // 4):
        mask = jnp.where(row == b, jnp.broadcast_to(by_row[b:b + 1, :], (CY, NZ)), mask)
    mask_ref[pl.ds(0, CY), :] = mask

    def rate(k):
        halves = sum(1 for v in VELOCITIES[k] if v > 0)
        return rates_ref[k] * np.float32(0.5 ** halves)

    def moved(source, i, layer, half):
        a, b, c = VELOCITIES[i]
        value = source[a, b, c, layer + 2 - a, pl.ds(TOP + 8 * half + 1 - b, 8), :]
        return value if c == 1 else pltpu.roll(value, (c - 1) % NZ, 1)

    def collide_layer(layer, source, target):
        for half in range(2):
            rows = pl.ds(8 * half, 8)
            if source is None:
                f = [pop_ref[i, layer, rows, :] for i in range(27)]
            else:
                f = [moved(source, i, layer, half) for i in range(27)]
            for v, value in zip(VELOCITIES, collide(f, mask_ref[rows, :] > 0.5, rate)):
                target[v[0], v[1], v[2], layer + 1, pl.ds(TOP + 8 * half, 8), :] = value

    def halo(step, n):
        dx, dy = HALO[n]
        buf, deep = (coll0, 2) if step == 0 else (coll1, 1)
        sx, lx = {1: (CX, 0), -1: (1, CX + 1), 0: (pl.ds(1, CX),) * 2}[dx]
        sy, ly = {1: (TOP + CY - deep, TOP - deep), -1: (TOP, TOP + CY), 0: (TOP,) * 2}[dy]
        rows = CY if dy == 0 else deep
        a = {1: pl.ds(2, 1), -1: pl.ds(0, 1), 0: slice(None)}[dx]
        b = {1: pl.ds(3 - deep, deep), -1: pl.ds(0, deep), 0: slice(None)}[dy]
        return pltpu.make_async_remote_copy(
            buf.at[a, b, :, sx, pl.ds(sy, rows)], buf.at[a, b, :, lx, pl.ds(ly, rows)],
            halo_send.at[step, n], halo_recv.at[step, n], device_id=beside(dx, dy), device_id_type=LOGICAL)

    def mask_row(n):
        dy = HALO[n][1]
        return pltpu.make_async_remote_copy(
            mask_ref.at[pl.ds(CY - 1 if dy > 0 else 0, 1)], mask_ref.at[pl.ds(CY if dy > 0 else CY + 1, 1)],
            halo_send.at[1, n], halo_recv.at[1, n], device_id=beside(0, dy), device_id_type=LOGICAL)

    def collide_edges():
        f = []
        for a, b, c in VELOCITIES:
            value = jnp.concatenate(
                [coll0[a, b, c, layer + 2 - a, pl.ds(TOP - b, 2, stride=CY + 1), :] for layer in range(CX)], axis=0)
            f.append(value if c == 1 else pltpu.roll(value, (c - 1) % NZ, 1))
        solid = jnp.concatenate([mask_ref[pl.ds(CY, 2), :]] * CX, axis=0)
        for (a, b, c), value in zip(VELOCITIES, collide(f, solid > 0.5, rate)):
            if b != 1:
                side = 0 if b == 2 else 1
                for layer in range(CX):
                    row = 2 * layer + side
                    coll1[a, b, c, layer + 1, pl.ds(TOP + CY if side else TOP - 1, 1), :] = value[row:row + 1]

    def sweep(layers, body):
        def once(t, _):
            body(layers(t))
            return 0
        lax.fori_loop(0, 2, once, 0)

    outer, inner = lambda t: 3 * t, lambda t: 1 + t

    for n in (0, 3):
        loads[n].wait()
    sweep(outer, lambda layer: collide_layer(layer, None, coll0))
    pl.semaphore_wait(barrier, len(SIDE_X) + len(PLANE) + len(COLUMN))
    for n in SIDE_X:
        halo(0, n).start()
    for k in sorted(COLUMN, key=lambda k: -hops(k)):
        pl.semaphore_signal(joined, inc=1, device_id=place(k), device_id_type=LOGICAL)
    for n in (1, 2):
        loads[n].wait()
    sweep(inner, lambda layer: collide_layer(layer, None, coll0))
    for n in SIDE_Y:
        mask_row(n).start()
        halo(0, n).start()

    for n in (6, 7, 8):
        loads[n].wait()
    owner_row = jnp.broadcast_to(owners_ref[...], (N_DEV, N_DEV))
    owner_col = owner_row.T
    sub = lax.broadcasted_iota(jnp.int32, (N_DEV, N_DEV), 0)
    lane = lax.broadcasted_iota(jnp.int32, (N_DEV, N_DEV), 1)
    rank = jnp.sum(jnp.where((owner_row == owner_col) & (sub < lane), 1.0, 0.0), axis=0, keepdims=True)
    code = (bricks_ref[...] + 128 * levels_ref[...] - 127).astype(F32)
    for slot in range(2):
        named = jnp.where((owner_row == sub) & (rank == slot), jnp.broadcast_to(code, (N_DEV, N_DEV)), 0.0)
        taken = (4.0 * jnp.sum(named, axis=1, keepdims=True) - 4.0).astype(jnp.int32)
        for part in range(8):
            number = lane + 128 * part
            for zz in range(4):
                pick[pl.ds((zz * 2 + slot) * 128, 128), pl.ds(part * 128, 128)] = jnp.where(
                    number == taken + zz, 1.0, 0.0).astype(BF16)
    fine[:, :, :, pl.ds(216, 40), :] = jnp.zeros((2, 2, 4, 40, NZ), F32)

    for n in SIDE_Y:
        mask_row(n).wait_recv()
        halo(0, n).wait_recv()
    sweep(inner, lambda layer: collide_layer(layer, coll0, coll1))
    from_far = s % 4 == 0

    def arrive(swapped):
        def wait(dx):
            for n in SIDE_X:
                if HALO[n][0] == dx:
                    halo(0, n).wait_recv()

        @pl.when(from_far != swapped)
        def _():
            wait(-1)

        @pl.when(from_far == swapped)
        def _():
            wait(1)

    near = jnp.where(from_far, CX - 1, 0)
    arrive(False)
    collide_layer(near, coll0, coll1)
    arrive(True)
    collide_layer(CX - 1 - near, coll0, coll1)
    for n in SIDE_X:
        halo(1, n).start()
    collide_edges()

    tau = 1.0 / jnp.full((8, NZ), rates_ref[12], F32)
    factors = [(0.5 + h * (tau - 0.5)) / (h * tau) for h in (2.0, 4.0)]

    def finish(layer, side, which):
        for half in range(2):
            f = [moved(coll1, i, layer, half) for i in range(27)]
            for i in range(27):
                final[i, layer, pl.ds(8 * half, 8), :] = f[i]
            for level, values in enumerate(rescaled(f, factors)):
                for i in range(27):
                    for quarter in range(2):
                        fine[side, level, 2 * half + quarter, pl.ds(i * 8 + which * 4, 4), :] = values[i][4 * quarter:4 * quarter + 4]

    lanes = lax.broadcasted_iota(jnp.int32, (N_DEV, 128), 1)
    dims = (((1,), (1,)), ((), ()))

    def send(part):
        for k in FAR:
            to = place(k)
            pltpu.make_async_remote_copy(
                out_buf.at[PARTS[part], to], got_ref.at[PARTS[part], me],
                far_send.at[part], far_recv.at[part], device_id=to, device_id_type=LOGICAL).start()
        pltpu.make_async_copy(out_buf.at[PARTS[part], me], got_ref.at[PARTS[part], me], far_recv.at[part]).start()

    def hand_over(side):
        for level in range(2):
            for b in range(4):
                value = fine[side, level, b]
                top = value.astype(BF16)
                columns = pl.ds((level * 4 + b) * NZ, NZ)
                table_hi[:, columns] = top
                table_lo[:, columns] = (value - top.astype(F32)).astype(BF16)
        for zz in range(4):
            chosen = pick[pl.ds(zz * 256, 256), :]
            got = lax.dot_general(chosen, table_hi[...], dims, preferred_element_type=F32)
            got = got + lax.dot_general(chosen, table_lo[...], dims, preferred_element_type=F32)
            for slot in range(2):
                value = got[128 * slot:128 * slot + 128]
                out_buf[whole(side, zz, slot)] = value[:, 0:128]
                place_at = 88 * (side * 8 + zz * 2 + slot)
                chunk, start = place_at // 128, place_at % 128
                turned = value[:, 128:256]
                if start:
                    turned = pltpu.roll(turned, start, 1)
                    out_buf[mixed(chunk)] = jnp.where(lanes < start, out_buf[mixed(chunk)], turned)
                else:
                    out_buf[mixed(chunk)] = turned
                if start + 88 > 128:
                    out_buf[mixed(chunk + 1)] = turned
            if 4 * side + zz in ENDS:
                send(ENDS.index(4 * side + zz))

    finish(1, 0, 0)
    finish(2, 0, 1)
    pl.semaphore_wait(joined, len(COLUMN))
    hand_over(0)
    for n in SIDE_X:
        halo(1, n).wait_recv()
    finish(0, 1, 0)
    finish(3, 1, 1)
    keep = pltpu.make_async_copy(final, adv_ref, adv_sem)
    keep.start()
    hand_over(1)

    for n in SIDE_X:
        halo(0, n).wait_send()
        halo(1, n).wait_send()
    for n in SIDE_Y:
        halo(0, n).wait_send()
        mask_row(n).wait_send()
    keep.wait()
    for part in range(len(PARTS)):
        pltpu.make_async_copy(out_buf.at[PARTS[part]], got_ref.at[PARTS[part]], far_recv.at[part]).wait()
        rest = pl.ds(0, N_DEV - 1)
        pltpu.make_async_copy(out_buf.at[PARTS[part], rest], got_ref.at[PARTS[part], rest], far_send.at[part]).wait()


FAR = others()
PLANE = [k << 2 for k in range(1, 16)]
COLUMN = [k for k in range(1, N_DEV) if not k & 60]
HALO = [(1, 0), (-1, 0), (1, 1), (1, -1), (-1, 1), (-1, -1), (0, 1), (0, -1)]
SIDE_X = [0, 1, 2, 3, 4, 5]
SIDE_Y = [6, 7]
ENDS = [1, 3, 7]
NUMBER = {}
FIRST = [0]
for steps in zip([0] + [end + 1 for end in ENDS], ENDS):
    group = [("whole", step, slot) for step in range(steps[0], steps[1] + 1) for slot in range(2)]
    group += [("mixed", n) for n in range(176 * steps[0] // 128, 176 * (steps[1] + 1) // 128)]
    NUMBER.update({name: FIRST[-1] + n for n, name in enumerate(group)})
    FIRST.append(FIRST[-1] + len(group))
PARTS = [pl.ds(a, b - a) for a, b in zip(FIRST, FIRST[1:])]


def whole(side, zz, slot):
    return NUMBER["whole", 4 * side + zz, slot]


def mixed(n):
    return NUMBER["mixed", n]


def arrange(adv_ref, got_hbm, adv_out, ghosts_hbm, got_ref, ghosts_ref, kept_ref, keep_sem, load_sem, store_sem):
    pieces = [pl.ds(0, 6), pl.ds(6, 7), pl.ds(13, 7), pl.ds(20, 7)]
    loads = [pltpu.make_async_copy(got_hbm.at[rows], got_ref.at[rows], load_sem.at[n]) for n, rows in enumerate(pieces)]
    for load in loads:
        load.start()
    fetch = pltpu.make_async_copy(adv_ref, kept_ref, keep_sem.at[0])
    fetch.start()

    def put(eight, i, side, zz, slot):
        base = slot * 1728 + i * 64 + zz
        if side == 0:
            ghosts_ref[pl.ds(base + 16, 8, stride=4), :] = eight
        else:
            ghosts_ref[pl.ds(base, 4, stride=4), :] = eight[0:4]
            ghosts_ref[pl.ds(base + 48, 4, stride=4), :] = eight[4:8]

    def store(n, first, length):
        rows = pl.ds(first, length)
        stores.append(pltpu.make_async_copy(ghosts_ref.at[rows], ghosts_hbm.at[rows], store_sem.at[n]))
        stores[-1].start()

    for load in loads:
        load.wait()
    stores = []
    for slot in range(2):
        for side in range(2):
            for zz in range(4):
                turned = got_ref[whole(side, zz, slot)].T
                for i in range(16):
                    put(turned[8 * i:8 * i + 8], i, side, zz, slot)
        store(slot, slot * 1728, 1024)
    fetch.wait()
    stores.append(pltpu.make_async_copy(kept_ref, adv_out, keep_sem.at[1]))
    stores[-1].start()
    for n in range(11):
        turned = got_ref[mixed(n)].T
        for row in range(16):
            entry, i = (16 * n + row) // 11, 16 + (16 * n + row) % 11
            put(turned[8 * row:8 * row + 8], i, entry // 8, entry % 8 // 2, entry % 2)
    for slot in range(2):
        store(2 + slot, slot * 1728 + 1024, 704)
    for copy in stores:
        copy.wait()


def per_device(populations, moment_rates, solid_bricks, owners, bricks, levels):
    hbm = pl.BlockSpec(memory_space=pl.ANY)
    padded = (3, 3, 3, CX + 2, CY + 16, NZ)
    adv, got = pl.pallas_call(
        advance,
        out_shape=(jax.ShapeDtypeStruct((27, CX, CY, NZ), F32), jax.ShapeDtypeStruct((CHUNKS, N_DEV, 128), F32)),
        in_specs=[hbm] * 6,
        out_specs=(hbm, hbm),
        scratch_shapes=[
            pltpu.VMEM((27, CX, CY, NZ), F32),
            pltpu.SMEM((27,), F32),
            pltpu.VMEM((4, 32), jnp.int32),
            pltpu.VMEM((1, 128), jnp.int32),
            pltpu.VMEM((1, 128), jnp.int32),
            pltpu.VMEM((1, 128), jnp.int32),
            pltpu.VMEM(padded, F32),
            pltpu.VMEM(padded, F32),
            pltpu.VMEM((27, CX, CY, NZ), F32),
            pltpu.VMEM((CY + 8, NZ), F32),
            pltpu.VMEM((1024, 1024), BF16),
            pltpu.VMEM((2, 2, 4, 256, NZ), F32),
            pltpu.VMEM((256, 1024), BF16),
            pltpu.VMEM((256, 1024), BF16),
            pltpu.VMEM((CHUNKS, N_DEV, 128), F32),
            pltpu.SemaphoreType.DMA((CX + 5,)),
            pltpu.SemaphoreType.DMA((2, 8)),
            pltpu.SemaphoreType.DMA((2, 8)),
            pltpu.SemaphoreType.DMA,
            pltpu.SemaphoreType.DMA((len(PARTS),)),
            pltpu.SemaphoreType.DMA((len(PARTS),)),
            pltpu.SemaphoreType.REGULAR,
        ],
        compiler_params=pltpu.CompilerParams(collective_id=0, has_side_effects=True, vmem_limit_bytes=60 << 20),
        name="advance",
    )(populations, moment_rates, solid_bricks.reshape(4, 32), owners.reshape(1, 128), bricks.reshape(1, 128), levels.reshape(1, 128))
    adv, ghosts = pl.pallas_call(
        arrange,
        out_shape=(jax.ShapeDtypeStruct((27, CX, CY, NZ), F32), jax.ShapeDtypeStruct((2 * 1728, N_DEV), F32)),
        in_specs=[hbm, hbm],
        out_specs=(hbm, hbm),
        scratch_shapes=[
            pltpu.VMEM((CHUNKS, N_DEV, 128), F32),
            pltpu.VMEM((2 * 1728, N_DEV), F32),
            pltpu.VMEM((27, CX, CY, NZ), F32),
            pltpu.SemaphoreType.DMA((2,)),
            pltpu.SemaphoreType.DMA((4,)),
            pltpu.SemaphoreType.DMA((4,)),
        ],
        compiler_params=pltpu.CompilerParams(vmem_limit_bytes=60 << 20),
        name="arrange",
    )(adv, got)
    return adv, ghosts.reshape(2, 1728, N_DEV).transpose(2, 0, 1)


def solution(mesh):
    return jax.shard_map(
        per_device,
        mesh=mesh,
        in_specs=(
            P(None, "stream", "depth", None),
            P(),
            P("stream", "depth", None),
            P(("stream", "depth"), None),
            P(("stream", "depth")),
            P(("stream", "depth")),
        ),
        out_specs=(P(None, "stream", "depth", None), P(("stream", "depth"), None, None)),
        check_vma=False,
    )
```

```python
import itertools
import random

import jax
import jax.numpy as jnp
import numpy as np
from jax import lax
from jax.experimental import pallas as pl
from jax.experimental.pallas import tpu as pltpu
from jax.sharding import PartitionSpec as P

LOGICAL = pl.DeviceIdType.LOGICAL
F32 = jnp.float32
BF16 = jnp.bfloat16

N_STREAM = 32
N_DEPTH = 4
N_DEV = N_STREAM * N_DEPTH
CX = 4
CY = 16
NZ = 128
TOP = 8
CHUNKS = 27

line = np.array([1.0 / 6.0, 2.0 / 3.0, 1.0 / 6.0])
power_table = np.array([[1.0, 1.0, 1.0], [-1.0, 0.0, 1.0], [1.0, 0.0, 1.0]])
VELOCITIES = list(itertools.product(range(3), repeat=3))


def equilibrium_terms():
    rows = []
    for a, b, c in VELOCITIES:
        w = line[a] * line[b] * line[c]
        x, y, z = a - 1.0, b - 1.0, c - 1.0
        square = [4.5 * x * x - 1.5, 4.5 * y * y - 1.5, 4.5 * z * z - 1.5]
        rows.append([w * t for t in [1.0, 3 * x, 3 * y, 3 * z] + square + [9 * x * y, 9 * x * z, 9 * y * z]])
    rows = np.array(rows)
    moments = np.kron(np.kron(power_table, power_table), power_table) @ rows
    return rows, np.where(np.abs(moments) < 1e-12, 0.0, moments)


GEQ_TERMS, MOMENT_TERMS = equilibrium_terms()


def combine(coefficients, basis):
    groups = {}
    for value, term in zip(coefficients, basis):
        if value != 0.0:
            groups.setdefault(round(float(value), 12), []).append(term)
    total = None
    for value, terms in groups.items():
        part = terms[0]
        for term in terms[1:]:
            part = part + term
        if value != 1.0:
            part = part * np.float32(value)
        total = part if total is None else total + part
    return total


def along(values, step):
    for axis in (2, 1, 0):
        out = {}
        for key in values:
            if key[axis] == 0:
                keys = [key[:axis] + (j,) + key[axis + 1:] for j in range(3)]
                for k, v in zip(keys, step(*[values[k] for k in keys])):
                    out[k] = v
        values = out
    return values


def to_moments(f0, f1, f2):
    ends = f0 + f2
    return ends + f1, f2 - f0, ends


def from_moments(m0, h1, h2):
    return h2 - h1, m0 - (h2 + h2), h2 + h1


def collide(f, solid, rate):
    moments = along(dict(zip(VELOCITIES, f)), to_moments)
    rho, jx, jy, jz = moments[0, 0, 0], moments[1, 0, 0], moments[0, 1, 0], moments[0, 0, 1]
    inverse = 1.0 / rho
    ux, uy, uz = jx * inverse, jy * inverse, jz * inverse
    basis = [rho, rho * ux, rho * uy, rho * uz, jx * ux, jy * uy, jz * uz, jx * uy, jx * uz, jy * uz]
    change = {}
    for k, key in enumerate(VELOCITIES):
        balance = combine(MOMENT_TERMS[k], basis)
        excess = moments[key] if balance is None else moments[key] - balance
        change[key] = excess * rate(k)
    change = along(change, from_moments)
    return [jnp.where(solid, f[26 - i], f[i] - change[key]) for i, key in enumerate(VELOCITIES)]


def rescaled(f, factors):
    rho = f[0]
    for value in f[1:]:
        rho = rho + value
    speeds = []
    for axis in range(3):
        up = [f[i] for i, v in enumerate(VELOCITIES) if v[axis] == 2]
        down = [f[i] for i, v in enumerate(VELOCITIES) if v[axis] == 0]
        total = up[0]
        for value in up[1:]:
            total = total + value
        for value in down:
            total = total - value
        speeds.append(total)
    inverse = 1.0 / rho
    jx, jy, jz = speeds
    ux, uy, uz = jx * inverse, jy * inverse, jz * inverse
    xx, yy, zz = jx * ux, jy * uy, jz * uz
    still = rho - 1.5 * (xx + yy + zz)
    out = [[None] * 27 for _ in factors]
    for i in range(14):
        a, b, c = (v - 1 for v in VELOCITIES[i])
        weight = np.float32(np.prod([line[v] for v in VELOCITIES[i]]))
        even, odd = still, None
        flow = None
        for sign, j, u in ((a, jx, ux), (b, jy, uy), (c, jz, uz)):
            if sign:
                flow = ((j, u) if sign > 0 else (-j, -u)) if flow is None else (
                    (flow[0] + j, flow[1] + u) if sign > 0 else (flow[0] - j, flow[1] - u))
        if flow is not None:
            even = still + 4.5 * (flow[0] * flow[1])
            odd = (3.0 * weight) * flow[0]
        even = even * weight
        for n, balance in ((i, even if odd is None else even + odd), (26 - i, even if odd is None else even - odd)):
            off = f[n] - balance
            for level, factor in enumerate(factors):
                out[level][n] = balance + factor * off
    return out


def hops(k):
    return sum((0, 1, 2, 1)[part] for part in ((k >> 2) & 3, (k >> 4) & 3, (k >> 1) & 1 | (k >> 5) & 2))


def others():
    every = list(range(1, N_DEV))
    random.Random(1).shuffle(every)
    every.sort(key=lambda k: -hops(k))
    return every


def advance(pop_hbm, rates_hbm, solid_hbm, owners_hbm, bricks_hbm, levels_hbm, adv_ref, got_ref,
            pop_ref, rates_ref, solid_ref, owners_ref, bricks_ref, levels_ref,
            coll0, coll1, final, mask_ref, pick, fine, table, out_buf,
            load_sem, halo_send, halo_recv, adv_sem, far_send, far_recv, joined):
    loads = [pltpu.make_async_copy(pop_hbm.at[:, layer], pop_ref.at[:, layer], load_sem.at[layer]) for layer in range(CX)]
    small = [(rates_hbm, rates_ref), (solid_hbm, solid_ref), (owners_hbm, owners_ref), (bricks_hbm, bricks_ref), (levels_hbm, levels_ref)]
    loads += [pltpu.make_async_copy(a, b, load_sem.at[CX + i]) for i, (a, b) in enumerate(small)]
    for n in (4, 5, 0, 3, 1, 2, 6, 7, 8):
        loads[n].start()
    s, p = lax.axis_index("stream"), lax.axis_index("depth")
    me = s * N_DEPTH + p
    flips = [(1 << b) * (1 - 2 * ((me // (1 << b)) % 2)) for b in range(7)]
    low, high = [0], [me]
    for b in range(3):
        low = low + [t + flips[b] for t in low]
    for b in range(3, 7):
        high = high + [t + flips[b] for t in high]

    def place(k):
        return high[k >> 3] + low[k & 7]

    def beside(dx, dy):
        return ((s + dx + N_STREAM) % N_STREAM) * N_DEPTH + (p + dy + N_DEPTH) % N_DEPTH

    barrier = pltpu.get_barrier_semaphore()
    for n in SIDE_X:
        pl.semaphore_signal(barrier, inc=1, device_id=beside(*HALO[n]), device_id_type=LOGICAL)
    for k in sorted(PLANE + COLUMN, key=lambda k: -hops(k)):
        pl.semaphore_signal(barrier, inc=1, device_id=place(k), device_id_type=LOGICAL)

    for n in (4, 5):
        loads[n].wait()
    spread = (lax.broadcasted_iota(jnp.int32, (32, NZ), 1) // 4 == lax.broadcasted_iota(jnp.int32, (32, NZ), 0)).astype(BF16)
    by_row = jnp.dot(solid_ref[...].astype(F32).astype(BF16), spread, preferred_element_type=F32)
    row = lax.broadcasted_iota(jnp.int32, (CY, NZ), 0) // 4
    mask = jnp.zeros((CY, NZ), F32)
    for b in range(CY // 4):
        mask = jnp.where(row == b, jnp.broadcast_to(by_row[b:b + 1, :], (CY, NZ)), mask)
    mask_ref[pl.ds(0, CY), :] = mask

    def rate(k):
        halves = sum(1 for v in VELOCITIES[k] if v > 0)
        return rates_ref[k] * np.float32(0.5 ** halves)

    def moved(source, i, layer, half):
        a, b, c = VELOCITIES[i]
        value = source[a, b, c, layer + 2 - a, pl.ds(TOP + 8 * half + 1 - b, 8), :]
        return value if c == 1 else pltpu.roll(value, (c - 1) % NZ, 1)

    def collide_layer(layer, source, target):
        for half in range(2):
            rows = pl.ds(8 * half, 8)
            if source is None:
                f = [pop_ref[i, layer, rows, :] for i in range(27)]
            else:
                f = [moved(source, i, layer, half) for i in range(27)]
            for v, value in zip(VELOCITIES, collide(f, mask_ref[rows, :] > 0.5, rate)):
                target[v[0], v[1], v[2], layer + 1, pl.ds(TOP + 8 * half, 8), :] = value

    def halo(step, n):
        dx, dy = HALO[n]
        buf, deep = (coll0, 2) if step == 0 else (coll1, 1)
        sx, lx = {1: (CX, 0), -1: (1, CX + 1), 0: (pl.ds(1, CX),) * 2}[dx]
        sy, ly = {1: (TOP + CY - deep, TOP - deep), -1: (TOP, TOP + CY), 0: (TOP,) * 2}[dy]
        rows = CY if dy == 0 else deep
        a = {1: pl.ds(2, 1), -1: pl.ds(0, 1), 0: slice(None)}[dx]
        b = {1: pl.ds(3 - deep, deep), -1: pl.ds(0, deep), 0: slice(None)}[dy]
        return pltpu.make_async_remote_copy(
            buf.at[a, b, :, sx, pl.ds(sy, rows)], buf.at[a, b, :, lx, pl.ds(ly, rows)],
            halo_send.at[step, n], halo_recv.at[step, n], device_id=beside(dx, dy), device_id_type=LOGICAL)

    def mask_row(n):
        dy = HALO[n][1]
        return pltpu.make_async_remote_copy(
            mask_ref.at[pl.ds(CY - 1 if dy > 0 else 0, 1)], mask_ref.at[pl.ds(CY if dy > 0 else CY + 1, 1)],
            halo_send.at[1, n], halo_recv.at[1, n], device_id=beside(0, dy), device_id_type=LOGICAL)

    def collide_edges():
        f = []
        for a, b, c in VELOCITIES:
            value = jnp.concatenate(
                [coll0[a, b, c, layer + 2 - a, pl.ds(TOP - b, 2, stride=CY + 1), :] for layer in range(CX)], axis=0)
            f.append(value if c == 1 else pltpu.roll(value, (c - 1) % NZ, 1))
        solid = jnp.concatenate([mask_ref[pl.ds(CY, 2), :]] * CX, axis=0)
        for (a, b, c), value in zip(VELOCITIES, collide(f, solid > 0.5, rate)):
            if b != 1:
                side = 0 if b == 2 else 1
                for layer in range(CX):
                    row = 2 * layer + side
                    coll1[a, b, c, layer + 1, pl.ds(TOP + CY if side else TOP - 1, 1), :] = value[row:row + 1]

    def sweep(layers, body):
        def once(t, _):
            body(layers(t))
            return 0
        lax.fori_loop(0, 2, once, 0)

    outer, inner = lambda t: 3 * t, lambda t: 1 + t

    for n in (0, 3):
        loads[n].wait()
    sweep(outer, lambda layer: collide_layer(layer, None, coll0))
    pl.semaphore_wait(barrier, len(SIDE_X) + len(PLANE) + len(COLUMN))
    for n in SIDE_X:
        halo(0, n).start()
    for k in sorted(COLUMN, key=lambda k: -hops(k)):
        pl.semaphore_signal(joined, inc=1, device_id=place(k), device_id_type=LOGICAL)
    for n in (1, 2):
        loads[n].wait()
    sweep(inner, lambda layer: collide_layer(layer, None, coll0))
    for n in SIDE_Y:
        mask_row(n).start()
        halo(0, n).start()

    for n in (6, 7, 8):
        loads[n].wait()
    owner_row = jnp.broadcast_to(owners_ref[...], (N_DEV, N_DEV))
    owner_col = owner_row.T
    sub = lax.broadcasted_iota(jnp.int32, (N_DEV, N_DEV), 0)
    lane = lax.broadcasted_iota(jnp.int32, (N_DEV, N_DEV), 1)
    rank = jnp.sum(jnp.where((owner_row == owner_col) & (sub < lane), 1.0, 0.0), axis=0, keepdims=True)
    code = (bricks_ref[...] + 128 * levels_ref[...] - 127).astype(F32)
    for slot in range(2):
        named = jnp.where((owner_row == sub) & (rank == slot), jnp.broadcast_to(code, (N_DEV, N_DEV)), 0.0)
        taken = (4.0 * jnp.sum(named, axis=1, keepdims=True) - 4.0).astype(jnp.int32)
        for part in range(8):
            number = lane + 128 * part
            for zz in range(4):
                pick[pl.ds((zz * 2 + slot) * 128, 128), pl.ds(part * 128, 128)] = jnp.where(
                    number == taken + zz, 1.0, 0.0).astype(BF16)
    fine[:, :, :, pl.ds(216, 40), :] = jnp.zeros((2, 2, 4, 40, NZ), F32)

    for n in SIDE_Y:
        mask_row(n).wait_recv()
        halo(0, n).wait_recv()
    sweep(inner, lambda layer: collide_layer(layer, coll0, coll1))
    from_far = s % 4 == 0

    def arrive(swapped):
        def wait(dx):
            for n in SIDE_X:
                if HALO[n][0] == dx:
                    halo(0, n).wait_recv()

        @pl.when(from_far != swapped)
        def _():
            wait(-1)

        @pl.when(from_far == swapped)
        def _():
            wait(1)

    near = jnp.where(from_far, CX - 1, 0)
    arrive(False)
    collide_layer(near, coll0, coll1)
    arrive(True)
    collide_layer(CX - 1 - near, coll0, coll1)
    for n in SIDE_X:
        halo(1, n).start()
    collide_edges()

    tau = 1.0 / jnp.full((8, NZ), rates_ref[12], F32)
    factors = [(0.5 + h * (tau - 0.5)) / (h * tau) for h in (2.0, 4.0)]

    def finish(layer, side, which):
        for half in range(2):
            f = [moved(coll1, i, layer, half) for i in range(27)]
            for i in range(27):
                final[i, layer, pl.ds(8 * half, 8), :] = f[i]
            for level, values in enumerate(rescaled(f, factors)):
                for i in range(27):
                    for quarter in range(2):
                        fine[side, level, 2 * half + quarter, pl.ds(i * 8 + which * 4, 4), :] = values[i][4 * quarter:4 * quarter + 4]

    lanes = lax.broadcasted_iota(jnp.int32, (N_DEV, 128), 1)
    dims = (((1,), (1,)), ((), ()))

    def send(part):
        for k in FAR:
            to = place(k)
            pltpu.make_async_remote_copy(
                out_buf.at[PARTS[part], to], got_ref.at[PARTS[part], me],
                far_send.at[part], far_recv.at[part], device_id=to, device_id_type=LOGICAL).start()
        pltpu.make_async_copy(out_buf.at[PARTS[part], me], got_ref.at[PARTS[part], me], far_recv.at[part]).start()

    def hand_over(side):
        for level in range(2):
            for b in range(4):
                value = fine[side, level, b]
                top = value.astype(BF16)
                columns = pl.ds((level * 4 + b) * NZ, NZ)
                table[:, columns] = top
                table[:, pl.ds((8 + level * 4 + b) * NZ, NZ)] = (value - top.astype(F32)).astype(BF16)
        for zz in range(4):
            chosen = pick[pl.ds(zz * 256, 256), :]
            got = lax.dot_general(jnp.concatenate([chosen, chosen], axis=1), table[...], dims, preferred_element_type=F32)
            for slot in range(2):
                value = got[128 * slot:128 * slot + 128]
                out_buf[whole(side, zz, slot)] = value[:, 0:128]
                place_at = 88 * (side * 8 + zz * 2 + slot)
                chunk, start = place_at // 128, place_at % 128
                turned = value[:, 128:256]
                if start:
                    turned = pltpu.roll(turned, start, 1)
                    out_buf[mixed(chunk)] = jnp.where(lanes < start, out_buf[mixed(chunk)], turned)
                else:
                    out_buf[mixed(chunk)] = turned
                if start + 88 > 128:
                    out_buf[mixed(chunk + 1)] = turned
            if 4 * side + zz in ENDS:
                send(ENDS.index(4 * side + zz))

    finish(1, 0, 0)
    finish(2, 0, 1)
    pl.semaphore_wait(joined, len(COLUMN))
    hand_over(0)
    for n in SIDE_X:
        halo(1, n).wait_recv()
    finish(0, 1, 0)
    finish(3, 1, 1)
    keep = pltpu.make_async_copy(final, adv_ref, adv_sem)
    keep.start()
    hand_over(1)

    for n in SIDE_X:
        halo(0, n).wait_send()
        halo(1, n).wait_send()
    for n in SIDE_Y:
        halo(0, n).wait_send()
        mask_row(n).wait_send()
    keep.wait()
    for part in range(len(PARTS)):
        pltpu.make_async_copy(out_buf.at[PARTS[part]], got_ref.at[PARTS[part]], far_recv.at[part]).wait()
        rest = pl.ds(0, N_DEV - 1)
        pltpu.make_async_copy(out_buf.at[PARTS[part], rest], got_ref.at[PARTS[part], rest], far_send.at[part]).wait()


FAR = others()
PLANE = [k << 2 for k in range(1, 16)]
COLUMN = [k for k in range(1, N_DEV) if not k & 60]
HALO = [(1, 0), (-1, 0), (1, 1), (1, -1), (-1, 1), (-1, -1), (0, 1), (0, -1)]
SIDE_X = [0, 1, 2, 3, 4, 5]
SIDE_Y = [6, 7]
ENDS = [1, 3, 7]
NUMBER = {}
FIRST = [0]
for steps in zip([0] + [end + 1 for end in ENDS], ENDS):
    group = [("whole", step, slot) for step in range(steps[0], steps[1] + 1) for slot in range(2)]
    group += [("mixed", n) for n in range(176 * steps[0] // 128, 176 * (steps[1] + 1) // 128)]
    NUMBER.update({name: FIRST[-1] + n for n, name in enumerate(group)})
    FIRST.append(FIRST[-1] + len(group))
PARTS = [pl.ds(a, b - a) for a, b in zip(FIRST, FIRST[1:])]


def whole(side, zz, slot):
    return NUMBER["whole", 4 * side + zz, slot]


def mixed(n):
    return NUMBER["mixed", n]


def arrange(adv_ref, got_hbm, adv_out, ghosts_hbm, got_ref, ghosts_ref, kept_ref, keep_sem, load_sem, store_sem):
    pieces = [pl.ds(0, 6), pl.ds(6, 7), pl.ds(13, 7), pl.ds(20, 7)]
    loads = [pltpu.make_async_copy(got_hbm.at[rows], got_ref.at[rows], load_sem.at[n]) for n, rows in enumerate(pieces)]
    for load in loads:
        load.start()
    fetch = pltpu.make_async_copy(adv_ref, kept_ref, keep_sem.at[0])
    fetch.start()

    def put(eight, i, side, zz, slot):
        base = slot * 1728 + i * 64 + zz
        if side == 0:
            ghosts_ref[pl.ds(base + 16, 8, stride=4), :] = eight
        else:
            ghosts_ref[pl.ds(base, 4, stride=4), :] = eight[0:4]
            ghosts_ref[pl.ds(base + 48, 4, stride=4), :] = eight[4:8]

    def store(n, first, length):
        rows = pl.ds(first, length)
        stores.append(pltpu.make_async_copy(ghosts_ref.at[rows], ghosts_hbm.at[rows], store_sem.at[n]))
        stores[-1].start()

    for load in loads:
        load.wait()
    stores = []
    for slot in range(2):
        for side in range(2):
            for zz in range(4):
                turned = got_ref[whole(side, zz, slot)].T
                for i in range(16):
                    put(turned[8 * i:8 * i + 8], i, side, zz, slot)
        store(slot, slot * 1728, 1024)
    fetch.wait()
    stores.append(pltpu.make_async_copy(kept_ref, adv_out, keep_sem.at[1]))
    stores[-1].start()
    for n in range(11):
        turned = got_ref[mixed(n)].T
        for row in range(16):
            entry, i = (16 * n + row) // 11, 16 + (16 * n + row) % 11
            put(turned[8 * row:8 * row + 8], i, entry // 8, entry % 8 // 2, entry % 2)
    for slot in range(2):
        store(2 + slot, slot * 1728 + 1024, 704)
    for copy in stores:
        copy.wait()


def per_device(populations, moment_rates, solid_bricks, owners, bricks, levels):
    hbm = pl.BlockSpec(memory_space=pl.ANY)
    padded = (3, 3, 3, CX + 2, CY + 16, NZ)
    adv, got = pl.pallas_call(
        advance,
        out_shape=(jax.ShapeDtypeStruct((27, CX, CY, NZ), F32), jax.ShapeDtypeStruct((CHUNKS, N_DEV, 128), F32)),
        in_specs=[hbm] * 6,
        out_specs=(hbm, hbm),
        scratch_shapes=[
            pltpu.VMEM((27, CX, CY, NZ), F32),
            pltpu.SMEM((27,), F32),
            pltpu.VMEM((4, 32), jnp.int32),
            pltpu.VMEM((1, 128), jnp.int32),
            pltpu.VMEM((1, 128), jnp.int32),
            pltpu.VMEM((1, 128), jnp.int32),
            pltpu.VMEM(padded, F32),
            pltpu.VMEM(padded, F32),
            pltpu.VMEM((27, CX, CY, NZ), F32),
            pltpu.VMEM((CY + 8, NZ), F32),
            pltpu.VMEM((1024, 1024), BF16),
            pltpu.VMEM((2, 2, 4, 256, NZ), F32),
            pltpu.VMEM((256, 2048), BF16),
            pltpu.VMEM((CHUNKS, N_DEV, 128), F32),
            pltpu.SemaphoreType.DMA((CX + 5,)),
            pltpu.SemaphoreType.DMA((2, 8)),
            pltpu.SemaphoreType.DMA((2, 8)),
            pltpu.SemaphoreType.DMA,
            pltpu.SemaphoreType.DMA((len(PARTS),)),
            pltpu.SemaphoreType.DMA((len(PARTS),)),
            pltpu.SemaphoreType.REGULAR,
        ],
        compiler_params=pltpu.CompilerParams(collective_id=0, has_side_effects=True, vmem_limit_bytes=60 << 20),
        name="advance",
    )(populations, moment_rates, solid_bricks.reshape(4, 32), owners.reshape(1, 128), bricks.reshape(1, 128), levels.reshape(1, 128))
    adv, ghosts = pl.pallas_call(
        arrange,
        out_shape=(jax.ShapeDtypeStruct((27, CX, CY, NZ), F32), jax.ShapeDtypeStruct((2 * 1728, N_DEV), F32)),
        in_specs=[hbm, hbm],
        out_specs=(hbm, hbm),
        scratch_shapes=[
            pltpu.VMEM((CHUNKS, N_DEV, 128), F32),
            pltpu.VMEM((2 * 1728, N_DEV), F32),
            pltpu.VMEM((27, CX, CY, NZ), F32),
            pltpu.SemaphoreType.DMA((2,)),
            pltpu.SemaphoreType.DMA((4,)),
            pltpu.SemaphoreType.DMA((4,)),
        ],
        compiler_params=pltpu.CompilerParams(vmem_limit_bytes=60 << 20),
        name="arrange",
    )(adv, got)
    return adv, ghosts.reshape(2, 1728, N_DEV).transpose(2, 0, 1)


def solution(mesh):
    return jax.shard_map(
        per_device,
        mesh=mesh,
        in_specs=(
            P(None, "stream", "depth", None),
            P(),
            P("stream", "depth", None),
            P(("stream", "depth"), None),
            P(("stream", "depth")),
            P(("stream", "depth")),
        ),
        out_specs=(P(None, "stream", "depth", None), P(("stream", "depth"), None, None)),
        check_vma=False,
    )
```

```python
import itertools
import random

import jax
import jax.numpy as jnp
import numpy as np
from jax import lax
from jax.experimental import pallas as pl
from jax.experimental.pallas import tpu as pltpu
from jax.sharding import PartitionSpec as P

LOGICAL = pl.DeviceIdType.LOGICAL
F32 = jnp.float32
BF16 = jnp.bfloat16

N_STREAM = 32
N_DEPTH = 4
N_DEV = N_STREAM * N_DEPTH
CX = 4
CY = 16
NZ = 128
TOP = 8
CHUNKS = 27

line = np.array([1.0 / 6.0, 2.0 / 3.0, 1.0 / 6.0])
power_table = np.array([[1.0, 1.0, 1.0], [-1.0, 0.0, 1.0], [1.0, 0.0, 1.0]])
VELOCITIES = list(itertools.product(range(3), repeat=3))


def equilibrium_terms():
    rows = []
    for a, b, c in VELOCITIES:
        w = line[a] * line[b] * line[c]
        x, y, z = a - 1.0, b - 1.0, c - 1.0
        square = [4.5 * x * x - 1.5, 4.5 * y * y - 1.5, 4.5 * z * z - 1.5]
        rows.append([w * t for t in [1.0, 3 * x, 3 * y, 3 * z] + square + [9 * x * y, 9 * x * z, 9 * y * z]])
    rows = np.array(rows)
    moments = np.kron(np.kron(power_table, power_table), power_table) @ rows
    return rows, np.where(np.abs(moments) < 1e-12, 0.0, moments)


GEQ_TERMS, MOMENT_TERMS = equilibrium_terms()


def combine(coefficients, basis):
    groups = {}
    for value, term in zip(coefficients, basis):
        if value != 0.0:
            groups.setdefault(round(float(value), 12), []).append(term)
    total = None
    for value, terms in groups.items():
        part = terms[0]
        for term in terms[1:]:
            part = part + term
        if value != 1.0:
            part = part * np.float32(value)
        total = part if total is None else total + part
    return total


def along(values, step):
    for axis in (2, 1, 0):
        out = {}
        for key in values:
            if key[axis] == 0:
                keys = [key[:axis] + (j,) + key[axis + 1:] for j in range(3)]
                for k, v in zip(keys, step(*[values[k] for k in keys])):
                    out[k] = v
        values = out
    return values


def to_moments(f0, f1, f2):
    ends = f0 + f2
    return ends + f1, f2 - f0, ends


def from_moments(m0, h1, h2):
    return h2 - h1, m0 - (h2 + h2), h2 + h1


def collide(f, solid, rate):
    moments = along(dict(zip(VELOCITIES, f)), to_moments)
    rho, jx, jy, jz = moments[0, 0, 0], moments[1, 0, 0], moments[0, 1, 0], moments[0, 0, 1]
    inverse = 1.0 / rho
    ux, uy, uz = jx * inverse, jy * inverse, jz * inverse
    basis = [rho, rho * ux, rho * uy, rho * uz, jx * ux, jy * uy, jz * uz, jx * uy, jx * uz, jy * uz]
    change = {}
    for k, key in enumerate(VELOCITIES):
        balance = combine(MOMENT_TERMS[k], basis)
        excess = moments[key] if balance is None else moments[key] - balance
        change[key] = excess * rate(k)
    change = along(change, from_moments)
    return [jnp.where(solid, f[26 - i], f[i] - change[key]) for i, key in enumerate(VELOCITIES)]


def rescaled(f, factors):
    rho = f[0]
    for value in f[1:]:
        rho = rho + value
    speeds = []
    for axis in range(3):
        up = [f[i] for i, v in enumerate(VELOCITIES) if v[axis] == 2]
        down = [f[i] for i, v in enumerate(VELOCITIES) if v[axis] == 0]
        total = up[0]
        for value in up[1:]:
            total = total + value
        for value in down:
            total = total - value
        speeds.append(total)
    inverse = 1.0 / rho
    jx, jy, jz = speeds
    ux, uy, uz = jx * inverse, jy * inverse, jz * inverse
    xx, yy, zz = jx * ux, jy * uy, jz * uz
    still = rho - 1.5 * (xx + yy + zz)
    out = [[None] * 27 for _ in factors]
    for i in range(14):
        a, b, c = (v - 1 for v in VELOCITIES[i])
        weight = np.float32(np.prod([line[v] for v in VELOCITIES[i]]))
        even, odd = still, None
        flow = None
        for sign, j, u in ((a, jx, ux), (b, jy, uy), (c, jz, uz)):
            if sign:
                flow = ((j, u) if sign > 0 else (-j, -u)) if flow is None else (
                    (flow[0] + j, flow[1] + u) if sign > 0 else (flow[0] - j, flow[1] - u))
        if flow is not None:
            even = still + 4.5 * (flow[0] * flow[1])
            odd = (3.0 * weight) * flow[0]
        even = even * weight
        for n, balance in ((i, even if odd is None else even + odd), (26 - i, even if odd is None else even - odd)):
            off = f[n] - balance
            for level, factor in enumerate(factors):
                out[level][n] = balance + factor * off
    return out


def hops(k):
    return sum((0, 1, 2, 1)[part] for part in ((k >> 2) & 3, (k >> 4) & 3, (k >> 1) & 1 | (k >> 5) & 2))


def others():
    every = list(range(1, N_DEV))
    random.Random(1).shuffle(every)
    every.sort(key=lambda k: -hops(k))
    return every


def advance(pop_hbm, rates_hbm, solid_hbm, owners_hbm, bricks_hbm, levels_hbm, adv_ref, got_ref,
            pop_ref, rates_ref, solid_ref, owners_ref, bricks_ref, levels_ref,
            coll0, coll1, final, mask_ref, pick, fine, table, out_buf,
            load_sem, halo_send, halo_recv, adv_sem, far_send, far_recv, joined):
    loads = [pltpu.make_async_copy(pop_hbm.at[:, layer], pop_ref.at[:, layer], load_sem.at[layer]) for layer in range(CX)]
    small = [(rates_hbm, rates_ref), (solid_hbm, solid_ref), (owners_hbm, owners_ref), (bricks_hbm, bricks_ref), (levels_hbm, levels_ref)]
    loads += [pltpu.make_async_copy(a, b, load_sem.at[CX + i]) for i, (a, b) in enumerate(small)]
    for n in (4, 5, 0, 3, 1, 2, 6, 7, 8):
        loads[n].start()
    s, p = lax.axis_index("stream"), lax.axis_index("depth")
    me = s * N_DEPTH + p
    flips = [(1 << b) * (1 - 2 * ((me // (1 << b)) % 2)) for b in range(7)]
    low, high = [0], [me]
    for b in range(3):
        low = low + [t + flips[b] for t in low]
    for b in range(3, 7):
        high = high + [t + flips[b] for t in high]

    def place(k):
        return high[k >> 3] + low[k & 7]

    def beside(dx, dy):
        return ((s + dx + N_STREAM) % N_STREAM) * N_DEPTH + (p + dy + N_DEPTH) % N_DEPTH

    barrier = pltpu.get_barrier_semaphore()
    for n in SIDE_X:
        pl.semaphore_signal(barrier, inc=1, device_id=beside(*HALO[n]), device_id_type=LOGICAL)
    for k in sorted(PLANE + COLUMN, key=lambda k: -hops(k)):
        pl.semaphore_signal(barrier, inc=1, device_id=place(k), device_id_type=LOGICAL)

    for n in (4, 5):
        loads[n].wait()
    spread = (lax.broadcasted_iota(jnp.int32, (32, NZ), 1) // 4 == lax.broadcasted_iota(jnp.int32, (32, NZ), 0)).astype(BF16)
    by_row = jnp.dot(solid_ref[...].astype(F32).astype(BF16), spread, preferred_element_type=F32)
    row = lax.broadcasted_iota(jnp.int32, (CY, NZ), 0) // 4
    mask = jnp.zeros((CY, NZ), F32)
    for b in range(CY // 4):
        mask = jnp.where(row == b, jnp.broadcast_to(by_row[b:b + 1, :], (CY, NZ)), mask)
    mask_ref[pl.ds(0, CY), :] = mask

    def rate(k):
        halves = sum(1 for v in VELOCITIES[k] if v > 0)
        return rates_ref[k] * np.float32(0.5 ** halves)

    def moved(source, i, layer, half):
        a, b, c = VELOCITIES[i]
        value = source[a, b, c, layer + 2 - a, pl.ds(TOP + 8 * half + 1 - b, 8), :]
        return value if c == 1 else pltpu.roll(value, (c - 1) % NZ, 1)

    def collide_layer(layer, source, target):
        for half in range(2):
            rows = pl.ds(8 * half, 8)
            if source is None:
                f = [pop_ref[i, layer, rows, :] for i in range(27)]
            else:
                f = [moved(source, i, layer, half) for i in range(27)]
            for v, value in zip(VELOCITIES, collide(f, mask_ref[rows, :] > 0.5, rate)):
                target[v[0], v[1], v[2], layer + 1, pl.ds(TOP + 8 * half, 8), :] = value

    def halo(step, n):
        dx, dy = HALO[n]
        buf, deep = (coll0, 2) if step == 0 else (coll1, 1)
        sx, lx = {1: (CX, 0), -1: (1, CX + 1), 0: (pl.ds(1, CX),) * 2}[dx]
        sy, ly = {1: (TOP + CY - deep, TOP - deep), -1: (TOP, TOP + CY), 0: (TOP,) * 2}[dy]
        rows = CY if dy == 0 else deep
        a = {1: pl.ds(2, 1), -1: pl.ds(0, 1), 0: slice(None)}[dx]
        b = {1: pl.ds(3 - deep, deep), -1: pl.ds(0, deep), 0: slice(None)}[dy]
        return pltpu.make_async_remote_copy(
            buf.at[a, b, :, sx, pl.ds(sy, rows)], buf.at[a, b, :, lx, pl.ds(ly, rows)],
            halo_send.at[step, n], halo_recv.at[step, n], device_id=beside(dx, dy), device_id_type=LOGICAL)

    def mask_row(n):
        dy = HALO[n][1]
        return pltpu.make_async_remote_copy(
            mask_ref.at[pl.ds(CY - 1 if dy > 0 else 0, 1)], mask_ref.at[pl.ds(CY if dy > 0 else CY + 1, 1)],
            halo_send.at[1, n], halo_recv.at[1, n], device_id=beside(0, dy), device_id_type=LOGICAL)

    def collide_edges():
        f = []
        for a, b, c in VELOCITIES:
            value = jnp.concatenate(
                [coll0[a, b, c, layer + 2 - a, pl.ds(TOP - b, 2, stride=CY + 1), :] for layer in range(CX)], axis=0)
            f.append(value if c == 1 else pltpu.roll(value, (c - 1) % NZ, 1))
        solid = jnp.concatenate([mask_ref[pl.ds(CY, 2), :]] * CX, axis=0)
        for (a, b, c), value in zip(VELOCITIES, collide(f, solid > 0.5, rate)):
            if b != 1:
                side = 0 if b == 2 else 1
                for layer in range(CX):
                    row = 2 * layer + side
                    coll1[a, b, c, layer + 1, pl.ds(TOP + CY if side else TOP - 1, 1), :] = value[row:row + 1]

    def sweep(layers, body):
        def once(t, _):
            body(layers(t))
            return 0
        lax.fori_loop(0, 2, once, 0)

    outer, inner = lambda t: 3 * t, lambda t: 1 + t

    for n in (0, 3):
        loads[n].wait()
    sweep(outer, lambda layer: collide_layer(layer, None, coll0))
    pl.semaphore_wait(barrier, len(SIDE_X) + len(PLANE) + len(COLUMN))
    for n in SIDE_X:
        halo(0, n).start()
    for k in sorted(COLUMN, key=lambda k: -hops(k)):
        pl.semaphore_signal(joined, inc=1, device_id=place(k), device_id_type=LOGICAL)
    for n in (1, 2):
        loads[n].wait()
    sweep(inner, lambda layer: collide_layer(layer, None, coll0))
    for n in SIDE_Y:
        mask_row(n).start()
        halo(0, n).start()

    for n in (6, 7, 8):
        loads[n].wait()
    owner_row = jnp.broadcast_to(owners_ref[...], (N_DEV, N_DEV))
    owner_col = owner_row.T
    sub = lax.broadcasted_iota(jnp.int32, (N_DEV, N_DEV), 0)
    lane = lax.broadcasted_iota(jnp.int32, (N_DEV, N_DEV), 1)
    rank = jnp.sum(jnp.where((owner_row == owner_col) & (sub < lane), 1.0, 0.0), axis=0, keepdims=True)
    code = (bricks_ref[...] + 128 * levels_ref[...] - 127).astype(F32)
    for slot in range(2):
        named = jnp.where((owner_row == sub) & (rank == slot), jnp.broadcast_to(code, (N_DEV, N_DEV)), 0.0)
        taken = (4.0 * jnp.sum(named, axis=1, keepdims=True) - 4.0).astype(jnp.int32)
        for part in range(8):
            number = lane + 128 * part
            for zz in range(4):
                pick[pl.ds((zz * 2 + slot) * 128, 128), pl.ds(part * 128, 128)] = jnp.where(
                    number == taken + zz, 1.0, 0.0).astype(BF16)
    fine[:, :, :, pl.ds(216, 40), :] = jnp.zeros((2, 2, 4, 40, NZ), F32)

    for n in SIDE_Y:
        mask_row(n).wait_recv()
        halo(0, n).wait_recv()
    sweep(inner, lambda layer: collide_layer(layer, coll0, coll1))
    from_far = s % 4 == 0

    def arrive(swapped):
        def wait(dx):
            for n in SIDE_X:
                if HALO[n][0] == dx:
                    halo(0, n).wait_recv()

        @pl.when(from_far != swapped)
        def _():
            wait(-1)

        @pl.when(from_far == swapped)
        def _():
            wait(1)

    near = jnp.where(from_far, CX - 1, 0)
    arrive(False)
    collide_layer(near, coll0, coll1)
    arrive(True)
    collide_layer(CX - 1 - near, coll0, coll1)
    for n in SIDE_X:
        halo(1, n).start()
    collide_edges()

    tau = 1.0 / jnp.full((8, NZ), rates_ref[12], F32)
    factors = [(0.5 + h * (tau - 0.5)) / (h * tau) for h in (2.0, 4.0)]

    def finish(layer, side, which):
        for half in range(2):
            f = [moved(coll1, i, layer, half) for i in range(27)]
            for i in range(27):
                final[i, layer, pl.ds(8 * half, 8), :] = f[i]
            for level, values in enumerate(rescaled(f, factors)):
                for i in range(27):
                    for quarter in range(2):
                        fine[side, level, 2 * half + quarter, pl.ds(i * 8 + which * 4, 4), :] = values[i][4 * quarter:4 * quarter + 4]

    lanes = lax.broadcasted_iota(jnp.int32, (N_DEV, 128), 1)
    dims = (((1,), (1,)), ((), ()))

    def send(part):
        for k in FAR:
            to = place(k)
            pltpu.make_async_remote_copy(
                out_buf.at[PARTS[part], to], got_ref.at[PARTS[part], me],
                far_send.at[part], far_recv.at[part], device_id=to, device_id_type=LOGICAL).start()
        pltpu.make_async_copy(out_buf.at[PARTS[part], me], got_ref.at[PARTS[part], me], far_recv.at[part]).start()

    def hand_over(side):
        for level in range(2):
            for b in range(4):
                value = fine[side, level, b]
                top = value.astype(BF16)
                columns = pl.ds((level * 4 + b) * NZ, NZ)
                table[:, columns] = top
                table[:, pl.ds((8 + level * 4 + b) * NZ, NZ)] = (value - top.astype(F32)).astype(BF16)
        for zz in range(4):
            chosen = pick[pl.ds(zz * 256, 256), :]
            got = lax.dot_general(jnp.concatenate([chosen, chosen], axis=1), table[...], dims, preferred_element_type=F32)
            for slot in range(2):
                value = got[128 * slot:128 * slot + 128]
                out_buf[whole(side, zz, slot)] = value[:, 0:128]
                place_at = 88 * (side * 8 + zz * 2 + slot)
                chunk, start = place_at // 128, place_at % 128
                turned = value[:, 128:256]
                if start:
                    turned = pltpu.roll(turned, start, 1)
                    out_buf[mixed(chunk)] = jnp.where(lanes < start, out_buf[mixed(chunk)], turned)
                else:
                    out_buf[mixed(chunk)] = turned
                if start + 88 > 128:
                    out_buf[mixed(chunk + 1)] = turned
            if 4 * side + zz in ENDS:
                send(ENDS.index(4 * side + zz))

    finish(1, 0, 0)
    finish(2, 0, 1)
    pl.semaphore_wait(joined, len(COLUMN))
    hand_over(0)
    for n in SIDE_X:
        halo(1, n).wait_recv()
    finish(0, 1, 0)
    finish(3, 1, 1)
    keep = pltpu.make_async_copy(final, adv_ref, adv_sem)
    keep.start()
    hand_over(1)

    for n in SIDE_X:
        halo(0, n).wait_send()
        halo(1, n).wait_send()
    for n in SIDE_Y:
        halo(0, n).wait_send()
        mask_row(n).wait_send()
    keep.wait()
    for part in range(len(PARTS)):
        pltpu.make_async_copy(out_buf.at[PARTS[part]], got_ref.at[PARTS[part]], far_recv.at[part]).wait()
        rest = pl.ds(0, N_DEV - 1)
        pltpu.make_async_copy(out_buf.at[PARTS[part], rest], got_ref.at[PARTS[part], rest], far_send.at[part]).wait()


FAR = others()
PLANE = [k << 2 for k in range(1, 16)]
COLUMN = [k for k in range(1, N_DEV) if not k & 60]
HALO = [(1, 0), (-1, 0), (1, 1), (1, -1), (-1, 1), (-1, -1), (0, 1), (0, -1)]
SIDE_X = [0, 1, 2, 3, 4, 5]
SIDE_Y = [6, 7]
ENDS = [1, 3, 7]
NUMBER = {}
FIRST = [0]
for steps in zip([0] + [end + 1 for end in ENDS], ENDS):
    group = [("whole", step, slot) for step in range(steps[0], steps[1] + 1) for slot in range(2)]
    group += [("mixed", n) for n in range(176 * steps[0] // 128, 176 * (steps[1] + 1) // 128)]
    NUMBER.update({name: FIRST[-1] + n for n, name in enumerate(group)})
    FIRST.append(FIRST[-1] + len(group))
PARTS = [pl.ds(a, b - a) for a, b in zip(FIRST, FIRST[1:])]


def whole(side, zz, slot):
    return NUMBER["whole", 4 * side + zz, slot]


def mixed(n):
    return NUMBER["mixed", n]


def arrange(adv_ref, got_hbm, adv_out, ghosts_hbm, got_ref, ghosts_ref, kept_ref, keep_sem, load_sem, store_sem):
    pieces = [pl.ds(0, 6), pl.ds(6, 7), pl.ds(13, 7), pl.ds(20, 7)]
    loads = [pltpu.make_async_copy(got_hbm.at[rows], got_ref.at[rows], load_sem.at[n]) for n, rows in enumerate(pieces)]
    for n, load in enumerate(loads):
        load.start(priority=n % 2)
    fetch = pltpu.make_async_copy(adv_ref, kept_ref, keep_sem.at[0])
    fetch.start(priority=1)

    def put(eight, i, side, zz, slot):
        base = slot * 1728 + i * 64 + zz
        if side == 0:
            ghosts_ref[pl.ds(base + 16, 8, stride=4), :] = eight
        else:
            ghosts_ref[pl.ds(base, 4, stride=4), :] = eight[0:4]
            ghosts_ref[pl.ds(base + 48, 4, stride=4), :] = eight[4:8]

    def store(n, first, length):
        rows = pl.ds(first, length)
        stores.append(pltpu.make_async_copy(ghosts_ref.at[rows], ghosts_hbm.at[rows], store_sem.at[n]))
        stores[-1].start(priority=n % 2)

    for load in loads:
        load.wait()
    stores = []
    for slot in range(2):
        for side in range(2):
            for zz in range(4):
                turned = got_ref[whole(side, zz, slot)].T
                for i in range(16):
                    put(turned[8 * i:8 * i + 8], i, side, zz, slot)
        store(slot, slot * 1728, 1024)
    fetch.wait()
    stores.append(pltpu.make_async_copy(kept_ref, adv_out, keep_sem.at[1]))
    stores[-1].start()
    for n in range(11):
        turned = got_ref[mixed(n)].T
        for row in range(16):
            entry, i = (16 * n + row) // 11, 16 + (16 * n + row) % 11
            put(turned[8 * row:8 * row + 8], i, entry // 8, entry % 8 // 2, entry % 2)
    for slot in range(2):
        store(2 + slot, slot * 1728 + 1024, 704)
    for copy in stores:
        copy.wait()


def per_device(populations, moment_rates, solid_bricks, owners, bricks, levels):
    hbm = pl.BlockSpec(memory_space=pl.ANY)
    padded = (3, 3, 3, CX + 2, CY + 16, NZ)
    adv, got = pl.pallas_call(
        advance,
        out_shape=(jax.ShapeDtypeStruct((27, CX, CY, NZ), F32), jax.ShapeDtypeStruct((CHUNKS, N_DEV, 128), F32)),
        in_specs=[hbm] * 6,
        out_specs=(hbm, hbm),
        scratch_shapes=[
            pltpu.VMEM((27, CX, CY, NZ), F32),
            pltpu.SMEM((27,), F32),
            pltpu.VMEM((4, 32), jnp.int32),
            pltpu.VMEM((1, 128), jnp.int32),
            pltpu.VMEM((1, 128), jnp.int32),
            pltpu.VMEM((1, 128), jnp.int32),
            pltpu.VMEM(padded, F32),
            pltpu.VMEM(padded, F32),
            pltpu.VMEM((27, CX, CY, NZ), F32),
            pltpu.VMEM((CY + 8, NZ), F32),
            pltpu.VMEM((1024, 1024), BF16),
            pltpu.VMEM((2, 2, 4, 256, NZ), F32),
            pltpu.VMEM((256, 2048), BF16),
            pltpu.VMEM((CHUNKS, N_DEV, 128), F32),
            pltpu.SemaphoreType.DMA((CX + 5,)),
            pltpu.SemaphoreType.DMA((2, 8)),
            pltpu.SemaphoreType.DMA((2, 8)),
            pltpu.SemaphoreType.DMA,
            pltpu.SemaphoreType.DMA((len(PARTS),)),
            pltpu.SemaphoreType.DMA((len(PARTS),)),
            pltpu.SemaphoreType.REGULAR,
        ],
        compiler_params=pltpu.CompilerParams(collective_id=0, has_side_effects=True, vmem_limit_bytes=60 << 20),
        name="advance",
    )(populations, moment_rates, solid_bricks.reshape(4, 32), owners.reshape(1, 128), bricks.reshape(1, 128), levels.reshape(1, 128))
    adv, ghosts = pl.pallas_call(
        arrange,
        out_shape=(jax.ShapeDtypeStruct((27, CX, CY, NZ), F32), jax.ShapeDtypeStruct((2 * 1728, N_DEV), F32)),
        in_specs=[hbm, hbm],
        out_specs=(hbm, hbm),
        scratch_shapes=[
            pltpu.VMEM((CHUNKS, N_DEV, 128), F32),
            pltpu.VMEM((2 * 1728, N_DEV), F32),
            pltpu.VMEM((27, CX, CY, NZ), F32),
            pltpu.SemaphoreType.DMA((2,)),
            pltpu.SemaphoreType.DMA((4,)),
            pltpu.SemaphoreType.DMA((4,)),
        ],
        compiler_params=pltpu.CompilerParams(vmem_limit_bytes=60 << 20),
        name="arrange",
    )(adv, got)
    return adv, ghosts.reshape(2, 1728, N_DEV).transpose(2, 0, 1)


def solution(mesh):
    return jax.shard_map(
        per_device,
        mesh=mesh,
        in_specs=(
            P(None, "stream", "depth", None),
            P(),
            P("stream", "depth", None),
            P(("stream", "depth"), None),
            P(("stream", "depth")),
            P(("stream", "depth")),
        ),
        out_specs=(P(None, "stream", "depth", None), P(("stream", "depth"), None, None)),
        check_vma=False,
    )
```
